256 devices in a mesh: pool: 2 (over core), rep: 8 (over y_hi, x), tp: 16 (over z, y_lo).
Axes of the slice: x: 4, y: 4 (y_hi: 2, y_lo: 2; y = y_hi * 2 + y_lo), z: 8, core: 2. Of those that a mesh axis runs over, the one named last changes fastest.
Arguments:
- prompt_states: bfloat16 [2, 8, 1024, 8192], P('pool', 'rep', 'tp'), may hold values from -6 to 6
- w_query: bfloat16 [8192, 8192], P(None, 'tp'), may hold values from -9 to 9
- w_kv: bfloat16 [8192, 2048], P(None, 'tp'), may hold values from -0.0625 to 0.0625
- queries: bfloat16 [2, 8, 4, 64, 8192], P('pool', 'rep', None, None, 'tp'), may hold values from -110 to 110
- new_kv: bfloat16 [2, 8, 4, 64, 2048], P('pool', 'rep', None, None, 'tp'), may hold values from -6 to 6
- lengths: int32 [2, 8, 4], replicated, may hold values from 1 to 512, 1024 in all within a row
- pairing: int32 [2, 8], replicated, may hold values from 0 to 7, as said below
- assign: int32 [2, 8, 64], P('pool', 'rep'), may hold values from 0 to 3
- cache_len: int32 [2, 8, 64], P('pool', 'rep'), may hold values from 1 to 512
Outputs:
- prefill_out: bfloat16 [2, 8, 1024, 8192], P('pool', 'rep', None, 'tp')
- decode_out: bfloat16 [2, 8, 4, 64, 8192], P('pool', 'rep', None, None, 'tp')
The draws below stay inside these ranges and needn't reach their ends.
Inputs may be any that keep to these rules, and one draw needn't show every extreme that they name: Each pool's row of pairing is a permutation of 0 to 7 with pairing[p, 0] = 7 and pairing[p, d] = d for some d.
All inputs are finite; a program needn't handle non-finite values.
Results may differ from the reference program's by a relative error of at most 0.012.
The reference program's roundings to bfloat16 on the way count: a program that leaves them out, or rounds other values in their place, can miss the bound.
Values may be sent and summed in bfloat16 or wider, within the bound.
A program may use at most 128 MiB of HBM per device.

```python
import math
import jax
import jax.numpy as jnp
import numpy as np
from jax import lax

D = 8192
QH = 64
KVH = 8
HD = 128
GTOK = 1024
NP = 4
ROWS = 64
STEPS = 4
PMAX = 512
POOLS = 2
REPS = 8
N_POOL = 2
N_REP = 8


def draw_w_query(key, part):
    key = jax.random.fold_in(key, 11)
    base_key, scale_key = jax.random.split(key)
    base_draw = jnp.clip(jax.random.normal(base_key, (D, QH * HD), jnp.float32), -5.0, 5.0)
    head_scale = jnp.exp(jax.random.uniform(scale_key, (QH,), jnp.float32, 0.0, math.log(3.0)))
    column_scale = jnp.repeat(head_scale, HD) / math.sqrt(D)
    return (base_draw * column_scale[None, :]).astype(jnp.bfloat16)


def draw_queries(key, part):
    key = jax.random.fold_in(key, 23)
    base_key, scale_key = jax.random.split(key)
    shape_all = (POOLS, REPS, STEPS, ROWS, QH * HD)
    base_draw = jnp.clip(jax.random.normal(base_key, shape_all, jnp.float32), -4.0, 4.0)
    row_scale = jnp.exp(jax.random.uniform(scale_key, (POOLS, REPS, STEPS, ROWS, 1), jnp.float32, 0.0, math.log(4.0)))
    return (base_draw * row_scale).astype(jnp.bfloat16)


def pairing_row(key):
    perm_key, spot_key = jax.random.split(key)
    rest = jax.random.permutation(perm_key, REPS - 1).astype(jnp.int32)
    spot = jax.random.randint(spot_key, (), 1, REPS - 1).astype(jnp.int32)
    places = jnp.arange(REPS - 1, dtype=jnp.int32)
    target = spot - 1
    where_now = jnp.sum(jnp.where(rest == spot, places, 0)).astype(jnp.int32)
    displaced = jnp.sum(jnp.where(places == target, rest, 0)).astype(jnp.int32)
    swapped = jnp.where(places == target, spot, jnp.where(places == where_now, displaced, rest))
    head = jnp.full((1,), REPS - 1, jnp.int32)
    return jnp.concatenate([head, swapped.astype(jnp.int32)])


def draw_pairing(key, part):
    key = jax.random.fold_in(key, 37)
    rows_all = [pairing_row(jax.random.fold_in(key, pool_number)) for pool_number in range(POOLS)]
    return jnp.stack(rows_all, axis=0).astype(jnp.int32)


def plant(values, rng, smallest, largest):
    spot = [jax.random.randint(jax.random.fold_in(rng, axis), (), 0, length) for axis, length in enumerate(values.shape)]
    widest = values.shape.index(max(values.shape))
    neighbour = spot[:widest] + [(spot[widest] + 1) % values.shape[widest]] + spot[widest + 1:]
    return values.at[tuple(spot)].set(smallest).at[tuple(neighbour)].set(largest)


def shard_levels(own_key, shape, pieces, smallest, high):
    loudness, own = 1.0, jax.random.fold_in(own_key, 6)
    for axis_at, blocks in pieces:
        heights = jnp.exp(jax.random.uniform(jax.random.fold_in(own, axis_at), (blocks,), jnp.float32, smallest / len(pieces), high / len(pieces)))
        loudness = loudness * jnp.repeat(heights, shape[axis_at] // blocks).reshape([-1 if axis == axis_at else 1 for axis in range(len(shape))])
    return loudness


def length_profile(count, total, limit, slope):
    weights = [(1 << 20) // math.isqrt(rank ** slope) + 1 for rank in range(2, count + 1)]
    spare, holding = total - limit - (count - 1), [1] * (count - 1)
    while spare > 0:
        candidates = [i for i in range(count - 1) if holding[i] < limit]
        pool, remaining = sum([weights[i] for i in candidates]), spare
        for i in candidates:
            extra = min(limit - holding[i], max(1, remaining * weights[i] // pool), spare)
            holding[i] = holding[i] + extra
            spare = spare - extra
    return np.array([limit] + holding)


def ragged_sizes(key, number_of, total, limit, lean):
    if number_of == 2:
        one = jax.random.randint(key, (), max(1, total - limit), min(limit, total - 1) + 1)
        return jnp.stack([one, total - one])
    sizes = jnp.asarray(length_profile(number_of, total, limit, lean), jnp.int32)
    couples = (number_of - 1) // 2
    source_of, sink = sizes[1:1 + 2 * couples:2], sizes[2:2 + 2 * couples:2]
    room = jnp.minimum(source_of - 1, limit - sink)
    moved = jax.random.randint(jax.random.fold_in(key, 1), (couples,), 0, 1 << 20) % (room + 1)
    sizes = sizes.at[1:1 + 2 * couples:2].set(source_of - moved).at[2:2 + 2 * couples:2].set(sink + moved)
    return sizes[jax.random.permutation(jax.random.fold_in(key, 2), number_of)]


def centred(rng, shape, scale, reach, cuts=(), held_as=jnp.bfloat16):
    array = jax.random.normal(rng, shape, jnp.float32) * scale
    if len(cuts) > 0:
        array = shard_levels(rng, shape, cuts, -0.22, 0.18) * array
    return jnp.clip(array, min=-reach, max=reach).astype(held_as)


def setup_inputs(seed: int = 0) -> dict:
    key_list = jax.random.split(jax.random.key(seed), 10)
    prompt_states = centred(key_list[0], (POOLS, REPS, GTOK, D), 1.0, 6.0, ((0, 2), (1, 8), (2, 16)))
    w_query = draw_w_query(jax.random.fold_in(key_list[9], 71), 0)
    w_kv = centred(key_list[2], (D, 2 * KVH * HD), D ** -0.5, 0.0625, ((1, 16),))
    queries = draw_queries(jax.random.fold_in(key_list[9], 71), 0)
    new_kv = centred(key_list[4], (POOLS, REPS, STEPS, ROWS, 2 * KVH * HD), 1.0, 6.0, ((0, 2), (1, 8), (4, 16)))
    lengths = jax.vmap(lambda own: ragged_sizes(own, NP, GTOK, PMAX, 1))(jax.random.split(key_list[5], POOLS * REPS)).reshape((POOLS, REPS, NP)).astype(jnp.int32)
    pairing = draw_pairing(jax.random.fold_in(key_list[9], 71), 0)
    assign = plant(jax.random.randint(key_list[7], (POOLS, REPS, ROWS), 0, NP), jax.random.fold_in(key_list[7], 1), 0, NP - 1).astype(jnp.int32)
    cache_len = plant(jax.random.randint(key_list[8], (POOLS, REPS, ROWS), 1, PMAX + 1), jax.random.fold_in(key_list[8], 1), 1, PMAX).astype(jnp.int32)
    return dict(prompt_states=prompt_states, w_query=w_query, w_kv=w_kv, queries=queries, new_kv=new_kv, lengths=lengths, pairing=pairing, assign=assign, cache_len=cache_len)


theta_base = 500000.0
neg_large = -1e+30

def rotate(vectors, positions):
    half_dim = vectors.shape[-1] // 2
    inverse = theta_base ** (-(jnp.arange(half_dim, dtype=jnp.float32) / half_dim))
    angles = positions[:, None] * inverse[None, :]
    target = (positions.shape[0],) + (1,) * (vectors.ndim - 2) + (half_dim,)
    cosine = jnp.cos(angles).reshape(target)
    sine_term = jnp.sin(angles).reshape(target)
    former = vectors[..., :half_dim]
    latter = vectors[..., half_dim:]
    return jnp.concatenate([former * cosine - latter * sine_term, latter * cosine + former * sine_term], axis=-1)

def token_layout(lengths, token_count):
    span_ends = jnp.cumsum(lengths).astype(jnp.int32)
    starts = (span_ends - lengths).astype(jnp.int32)
    token_index = jnp.arange(token_count, dtype=jnp.int32)
    segment = lax.optimization_barrier(jnp.sum((token_index[:, None] >= span_ends[None, :]).astype(jnp.int32), axis=1)).astype(jnp.int32)
    member = segment[:, None] == jnp.arange(lengths.shape[0], dtype=jnp.int32)[None, :]
    anchor = lax.optimization_barrier(jnp.sum(jnp.where(member, starts[None, :], 0), axis=1)).astype(jnp.int32)
    return (segment, (token_index - anchor).astype(jnp.float32))

def decode_mask(lengths, row_assign, row_len, spots):
    starts = (jnp.cumsum(lengths) - lengths).astype(jnp.int32)
    member = row_assign[:, None] == jnp.arange(lengths.shape[0], dtype=jnp.int32)[None, :]
    lower = lax.optimization_barrier(jnp.sum(jnp.where(member, starts[None, :], 0), axis=1)).astype(jnp.int32)
    extent = lax.optimization_barrier(jnp.sum(jnp.where(member, lengths[None, :], 0), axis=1)).astype(jnp.int32)
    upper = lower + jnp.minimum(extent, row_len)
    return (spots[None, :] >= lower[:, None]) & (spots[None, :] < upper[:, None])

def prefill_attend(query, key_rows, value_rows, segment):
    token_count = query.shape[0]
    inv_root = 1.0 / math.sqrt(query.shape[-1])
    scores = jnp.einsum('qkgd,tkd->kgqt', query.astype(jnp.float32), key_rows.astype(jnp.float32)) * inv_root
    token_index = jnp.arange(token_count, dtype=jnp.int32)
    allowed = (segment[:, None] == segment[None, :]) & (token_index[None, :] <= token_index[:, None])
    scores = jnp.where(allowed, scores, neg_large)
    peak = lax.optimization_barrier(jnp.max(scores, axis=-1, keepdims=True))
    weights = jnp.where(allowed, jnp.exp(scores - peak), 0.0)
    rounded = (weights / lax.optimization_barrier(jnp.sum(weights, axis=-1, keepdims=True))).astype(jnp.bfloat16)
    mixed = jnp.einsum('kgqt,tkd->qkgd', rounded.astype(jnp.float32), value_rows.astype(jnp.float32))
    return mixed.astype(jnp.bfloat16).reshape(token_count, -1)

def prefill_group(states, lengths, w_query, w_kv):
    token_count = states.shape[0]
    segment, positions = token_layout(lengths, token_count)
    query = jnp.dot(states, w_query, preferred_element_type=jnp.float32).reshape(token_count, QH, HD)
    query = rotate(query, positions).astype(jnp.bfloat16)
    projected = jnp.dot(states, w_kv, preferred_element_type=jnp.float32).reshape(token_count, KVH, 2, HD)
    key_rows = rotate(projected[:, :, 0], positions).astype(jnp.bfloat16)
    value_rows = projected[:, :, 1].astype(jnp.bfloat16)
    attended = prefill_attend(query.reshape(token_count, KVH, QH // KVH, HD), key_rows, value_rows, segment)
    return (attended, key_rows, value_rows)

def decode_group(query_rows, new_rows, key_rows, value_rows, lengths, row_assign, row_len):
    steps_count = query_rows.shape[0]
    row_count = query_rows.shape[1]
    group_size = QH // KVH
    inv_root = 1.0 / math.sqrt(HD)
    query = query_rows.astype(jnp.float32).reshape(steps_count, row_count, KVH, group_size, HD)
    fresh = new_rows.astype(jnp.float32).reshape(steps_count, row_count, KVH, 2, HD)
    visible = decode_mask(lengths, row_assign, row_len, jnp.arange(key_rows.shape[0], dtype=jnp.int32))
    cache_scores = jnp.einsum('srkgd,tkd->srkgt', query, key_rows.astype(jnp.float32)) * inv_root
    own_scores = jnp.einsum('srkgd,urkd->srkgu', query, fresh[:, :, :, 0]) * inv_root
    step_index = jnp.arange(steps_count, dtype=jnp.int32)
    own_valid = (step_index[:, None] >= step_index[None, :])[:, None, None, None, :]
    cache_valid = visible[None, :, None, None, :]
    cache_scores = jnp.where(cache_valid, cache_scores, neg_large)
    own_scores = jnp.where(own_valid, own_scores, neg_large)
    peak = jnp.maximum(lax.optimization_barrier(jnp.max(cache_scores, axis=-1)), lax.optimization_barrier(jnp.max(own_scores, axis=-1)))[..., None]
    cache_weights = jnp.where(cache_valid, jnp.exp(cache_scores - peak), 0.0)
    own_weights = jnp.where(own_valid, jnp.exp(own_scores - peak), 0.0)
    total = lax.optimization_barrier(jnp.sum(cache_weights, axis=-1)) + lax.optimization_barrier(jnp.sum(own_weights, axis=-1))
    mixed = jnp.einsum('srkgt,tkd->srkgd', cache_weights, value_rows.astype(jnp.float32))
    mixed = mixed + jnp.einsum('srkgu,urkd->srkgd', own_weights, fresh[:, :, :, 1])
    return (mixed / total[..., None]).astype(jnp.bfloat16).reshape(steps_count, row_count, QH * HD)

def reference(prompt_states, w_query, w_kv, queries, new_kv, lengths, pairing, assign, cache_len):
    groups = N_POOL * N_REP
    flat_states = prompt_states.reshape(groups, GTOK, D)
    flat_lengths = lengths.reshape(groups, NP)

    def prefill_one(inputs_pair):
        return prefill_group(inputs_pair[0], inputs_pair[1], w_query, w_kv)
    attended, key_cache, value_cache = lax.map(prefill_one, (flat_states, flat_lengths))
    group_ids = jnp.arange(groups, dtype=jnp.int32)
    source = ((group_ids // N_REP + 1) % N_POOL * N_REP + pairing.reshape(groups)).astype(jnp.int32)

    def decode_one(inputs_tuple):
        anchor, query_rows, new_rows, row_assign, row_len = inputs_tuple
        key_rows = lax.dynamic_index_in_dim(key_cache, anchor, 0, keepdims=False)
        value_rows = lax.dynamic_index_in_dim(value_cache, anchor, 0, keepdims=False)
        source_lengths = lax.dynamic_index_in_dim(flat_lengths, anchor, 0, keepdims=False)
        return decode_group(query_rows, new_rows, key_rows, value_rows, source_lengths, row_assign, row_len)
    decoded = lax.map(decode_one, (source, queries.reshape(groups, STEPS, ROWS, QH * HD), new_kv.reshape(groups, STEPS, ROWS, 2 * KVH * HD), assign.reshape(groups, ROWS), cache_len.reshape(groups, ROWS)))
    return (attended.reshape(N_POOL, N_REP, GTOK, QH * HD), decoded.reshape(N_POOL, N_REP, STEPS, ROWS, QH * HD))
```

```python
import functools
import math

import jax
import jax.numpy as jnp
import numpy as np
from jax import lax
from jax.experimental import pallas as pl
from jax.experimental.pallas import tpu as pltpu
from jax.sharding import PartitionSpec as P

HD = 128
PLANES = 8
REPS = 8
HEADS = 4
TOK = 64
HALF = 32
PLANE_ROWS = 2 * TOK
WINDOW = 5
STEPS = 4
ROWS = 64
NEW = STEPS * ROWS
CACHE = PLANES * PLANE_ROWS
W_LOW = 2560
K_CHUNK = 2048

theta_base = 500000.0
neg_large = -1e30
exp_scale = math.log2(math.e) / math.sqrt(HD)


def remote(src, dst, send_sem, recv_sem, device):
    pltpu.make_async_remote_copy(
        src_ref=src,
        dst_ref=dst,
        send_sem=send_sem,
        recv_sem=recv_sem,
        device_id=device,
        device_id_type=pl.DeviceIdType.MESH,
    ).start()


def landed(ref, sem):
    pltpu.make_async_copy(ref, ref, sem).wait()


def softmax_mix(scores, values):
    peak = jnp.max(scores, axis=-1, keepdims=True)
    weights = jnp.exp2((scores - peak) * exp_scale)
    total = jnp.sum(weights, axis=-1, keepdims=True)
    mixed = jnp.dot(weights.astype(jnp.bfloat16), values, preferred_element_type=jnp.float32)
    return mixed / total


def scores_of(query, keys):
    return lax.dot_general(
        query, keys, (((1,), (1,)), ((), ())), preferred_element_type=jnp.float32
    )


def kernel(
    x_hbm,
    wq_hbm,
    wkv_hbm,
    queries_ref,
    new_ref,
    lengths_ref,
    pairing_ref,
    assign_ref,
    cache_len_ref,
    freq_ref,
    prefill_ref,
    decode_ref,
    xg,
    wq,
    wkv,
    acc,
    cos_t,
    sin_t,
    bias,
    qhome,
    qstage,
    kvhome,
    kvstage,
    p1,
    p2,
    dec,
    x0_sem,
    xs_send,
    w_sem,
    w_send,
    up_send,
    up_recv,
    down_send,
    down_recv,
    sib_send,
    sib_recv,
    new_send,
    new_recv,
    q_send,
    q_recv,
    kv_send,
    kv_send2,
    kv_recv,
    p1_send,
    p1_recv,
    p2_send,
    p2_recv,
):
    core = lax.axis_index("pool")
    rep = lax.axis_index("rep")
    t = lax.axis_index("tp")
    z = t // 2
    y = t % 2
    diag = core == y
    off = core != y
    other = 1 - core

    def dev(c2, g2, z2, y2):
        return (c2, g2, z2 * 2 + y2)

    up_dev = dev(core, rep, (z + 1) % PLANES, y)
    down_dev = dev(core, rep, (z + PLANES - 1) % PLANES, y)
    sibling = dev(other, rep, z, y)
    swap_low = dev(other, rep, z, 1 - y)
    swap_high = dev(other, (rep + REPS // 2) % REPS, z, 1 - y)
    across = dev(core, rep, z, 1 - y)
    row0 = pl.multiple_of(core * TOK, TOK)
    other_row0 = pl.multiple_of(other * TOK, TOK)

    wq_low = wq.at[pl.ds(0, W_LOW)]
    wq_high = wq.at[pl.ds(W_LOW, wq.shape[0] - W_LOW)]
    wq_hbm_low = wq_hbm.at[pl.ds(0, W_LOW)]
    wq_hbm_high = wq_hbm.at[pl.ds(W_LOW, wq.shape[0] - W_LOW)]

    def block(slot, half):
        return xg.at[slot, pl.ds(pl.multiple_of(row0 + half * HALF, HALF), HALF)]

    def sibling_block(slot, half):
        return xg.at[slot, pl.ds(pl.multiple_of(other_row0 + half * HALF, HALF), HALF)]

    @pl.when(diag)
    def _():
        for h in range(2):
            pltpu.make_async_copy(
                x_hbm.at[pl.ds(h * HALF, HALF)], block(0, h), x0_sem.at[h]
            ).start()
        pltpu.make_async_copy(wq_hbm_low, wq_low, w_sem.at[0]).start()
        pltpu.make_async_copy(wq_hbm_high, wq_high, w_sem.at[1]).start()
        pltpu.make_async_copy(wkv_hbm, wkv, w_sem.at[2]).start()

    barrier = pltpu.get_barrier_semaphore()

    def greet(n, carry):
        c2 = n // 16
        g2 = (n // 2) % 8
        y2 = n % 2
        mine = (c2 == core) & (g2 == rep) & (y2 == y)

        @pl.when(jnp.logical_not(mine))
        def _():
            pl.semaphore_signal(
                barrier, inc=1, device_id=dev(c2, g2, z, y2), device_id_type=pl.DeviceIdType.MESH
            )

        return carry

    lax.fori_loop(0, 32, greet, 0)
    for device in (up_dev, down_dev):
        pl.semaphore_signal(
            barrier, inc=1, device_id=device, device_id_type=pl.DeviceIdType.MESH
        )
    pl.semaphore_wait(barrier, 33)

    @pl.when(off)
    def _():
        for h in range(2):
            remote(
                x_hbm.at[pl.ds(h * HALF, HALF)],
                sibling_block(0, h),
                xs_send.at[h],
                x0_sem.at[h],
                swap_low,
            )
        remote(wq_hbm_high, wq_high, w_send.at[1], w_sem.at[1], swap_high)
        remote(wq_hbm_low, wq_low, w_send.at[0], w_sem.at[0], swap_low)
        remote(wkv_hbm, wkv, w_send.at[2], w_sem.at[2], swap_low)

    def send_up(src, dst, h, k):
        remote(block(src, h), block(dst, h), up_send.at[k], up_recv.at[k], up_dev)

    def send_down(src, dst, h, k):
        remote(block(src, h), block(dst, h), down_send.at[k], down_recv.at[k], down_dev)

    def share(slot, h):
        k = slot * 2 + h
        remote(block(slot, h), block(slot, h), sib_send.at[k], sib_recv.at[k], sibling)

    for h in range(2):
        landed(block(0, h), x0_sem.at[h])
        send_up(0, 1, h, h)
        send_down(0, 2, h, h)
        share(0, h)

    new_cols = pl.ds(CACHE, NEW)
    remote(new_ref, dec.at[y, new_cols], new_send.at[0], new_recv.at[0], across)
    dec[y, new_cols] = new_ref[...]

    def starts_of(rows, lens):
        end = jnp.int32(0)
        total = jnp.zeros_like(rows)
        for length in lens:
            end = end + length
            total = total + jnp.where(rows >= end, length, 0)
        return total

    work_lens = [lengths_ref[y, rep, j] for j in range(4)]
    home_lens = [lengths_ref[core, rep, j] for j in range(4)]
    paired = pairing_ref[core, rep]
    pair_lens = [lengths_ref[other, paired, j] for j in range(4)]

    def tables(plane, carry):
        rows = plane * PLANE_ROWS + lax.broadcasted_iota(jnp.int32, (PLANE_ROWS, HD), 0)
        lanes = lax.broadcasted_iota(jnp.int32, (PLANE_ROWS, HD), 1)
        offset = (rows - starts_of(rows, work_lens)).astype(jnp.float32)
        angle = offset * freq_ref[...]
        cos_t[plane] = jnp.cos(angle)
        sine = jnp.sin(angle)
        sin_t[plane] = jnp.where(lanes < HD // 2, -sine, sine)
        return carry

    lax.fori_loop(0, PLANES, tables, 0)

    def column(ref):
        spread = jnp.broadcast_to(ref[...], (ROWS, ROWS))
        here = lax.broadcasted_iota(jnp.int32, (ROWS, ROWS), 0) == lax.broadcasted_iota(
            jnp.int32, (ROWS, ROWS), 1
        )
        picked = jnp.where(here, spread.astype(jnp.float32), 0.0)
        return jnp.sum(picked, axis=1, keepdims=True).astype(jnp.int32)

    member = column(assign_ref)
    limit = column(cache_len_ref)
    lower = jnp.zeros_like(member)
    extent = jnp.zeros_like(member)
    begin = jnp.int32(0)
    for j in range(4):
        lower = jnp.where(member == j, begin, lower)
        extent = jnp.where(member == j, pair_lens[j], extent)
        begin = begin + pair_lens[j]
    upper = lower + jnp.minimum(extent, limit)
    spots = lax.broadcasted_iota(jnp.int32, (ROWS, CACHE), 1)
    visible = jnp.where((spots >= lower) & (spots < upper), 0.0, neg_large)
    new_spot = lax.broadcasted_iota(jnp.int32, (ROWS, NEW), 1)
    row = lax.broadcasted_iota(jnp.int32, (ROWS, NEW), 0)
    for s in range(STEPS):
        rows_here = pl.ds(s * ROWS, ROWS)
        bias[rows_here, pl.ds(0, CACHE)] = visible
        own = (new_spot % ROWS == row) & (new_spot // ROWS <= s)
        bias[rows_here, new_cols] = jnp.where(own, 0.0, neg_large)

    def relay(d, h):
        k = 2 * (d - 1) + h
        low, high = 2 * d - 1, 2 * d
        landed(block(low, h), up_recv.at[k])
        if d < 3:
            send_up(low, low + 2, h, k + 2)
        elif h == 0:
            send_up(low, low + 2, h, 6)
        share(low, h)
        landed(block(high, h), down_recv.at[k])
        if d < 3:
            send_down(high, high + 2, h, k + 2)
        elif h == 1:
            send_down(high, 7, h, 6)
        share(high, h)

    for d in (1, 2):
        for h in range(2):
            relay(d, h)
    relay(3, 0)
    landed(wq_low, w_sem.at[0])
    landed(wq_high, w_sem.at[1])
    landed(wkv, w_sem.at[2])

    def finish_plane(slot, plane, rows):
        cosine = cos_t[plane]
        sine = sin_t[plane]

        def turned(part):
            return part * cosine + pltpu.roll(part, HD // 2, 1) * sine

        heads = [turned(rows[:, h * HD : (h + 1) * HD]).astype(jnp.bfloat16) for h in range(HEADS)]
        raw = rows[:, HEADS * HD :]
        own = jnp.where(core == 0, turned(raw), raw).astype(jnp.bfloat16)
        kvstage[plane] = own

        @pl.when(diag)
        def _():
            for h in range(HEADS):
                qhome[plane, h] = heads[h]
            kvhome[core, plane] = own
            remote(
                kvstage.at[plane],
                kvhome.at[core, plane],
                kv_send.at[slot],
                kv_recv.at[core * PLANES + plane],
                across,
            )

        @pl.when(off)
        def _():
            for h in range(HEADS):
                qstage[slot, h] = heads[h]
            remote(
                kvstage.at[plane],
                kvhome.at[core, plane],
                kv_send.at[slot],
                kv_recv.at[core * PLANES + plane],
                swap_low,
            )
            remote(
                kvstage.at[plane],
                kvhome.at[core, plane],
                kv_send2.at[slot],
                kv_recv.at[core * PLANES + plane],
                sibling,
            )
            remote(qstage.at[slot], qhome.at[plane], q_send.at[slot], q_recv.at[plane], swap_low)

        @pl.when(plane == rep)
        def _():
            p1[rep] = own

        @pl.when(plane != rep)
        def _():
            remote(
                kvstage.at[plane],
                p1.at[rep],
                p1_send.at[slot],
                p1_recv.at[rep],
                dev(core, plane, z, y),
            )

    def project(b, carry):
        @pl.when(b == 2)
        def _():
            relay(3, 1)

        @pl.when(b == 3)
        def _():
            landed(block(7, 0), up_recv.at[6])
            share(7, 0)
            landed(block(7, 1), down_recv.at[6])
            share(7, 1)

        for j in range(2):
            for h in range(2):
                landed(sibling_block(2 * b + j, h), sib_recv.at[4 * b + 2 * j + h])

        acc[...] = jnp.zeros_like(acc)

        def step(k, inner):
            deep = pl.ds(pl.multiple_of(k * K_CHUNK, K_CHUNK), K_CHUNK)
            rows = xg[pl.ds(2 * b, 2), :, deep].reshape(2 * PLANE_ROWS, K_CHUNK)
            acc[:, : HEADS * HD] += jnp.dot(
                rows, wq[deep, :], preferred_element_type=jnp.float32
            )
            acc[:, HEADS * HD :] += jnp.dot(
                rows, wkv[deep, :], preferred_element_type=jnp.float32
            )
            return inner

        lax.fori_loop(0, wq.shape[0] // K_CHUNK, step, 0)
        finish_plane(2 * b, (z + b) % PLANES, acc[pl.ds(0, PLANE_ROWS), :])
        finish_plane(
            2 * b + 1, (z + 2 * PLANES - 1 - b) % PLANES, acc[pl.ds(PLANE_ROWS, PLANE_ROWS), :]
        )
        return carry

    lax.fori_loop(0, PLANES // 2, project, 0)

    for g2 in range(REPS):

        @pl.when(rep != g2)
        def _():
            landed(p1.at[g2], p1_recv.at[g2])

    cache_rows = pl.ds(pl.multiple_of(rep * PLANE_ROWS, PLANE_ROWS), PLANE_ROWS)

    def hand_over(d, carry):
        p2[d] = p1[pairing_ref[1 - y, d]]
        for y2 in range(2):
            mine = (1 - y == core) & (d == rep) & (y == y2)

            @pl.when(mine)
            def _():
                dec[core, cache_rows] = p2[d]

            @pl.when(jnp.logical_not(mine))
            def _():
                remote(
                    p2.at[d],
                    dec.at[core, cache_rows],
                    p2_send.at[2 * d + y2],
                    p2_recv.at[core * PLANES + rep],
                    dev(1 - y, d, z, y2),
                )

        return carry

    lax.fori_loop(0, REPS, hand_over, 0)

    for plane in range(PLANES):

        @pl.when(off)
        def _():
            landed(qhome.at[plane], q_recv.at[plane])
            landed(kvhome.at[0, plane], kv_recv.at[plane])
            landed(kvhome.at[1, plane], kv_recv.at[PLANES + plane])

        @pl.when(diag)
        def _():
            landed(kvhome.at[other, plane], kv_recv.at[other * PLANES + plane])

    def prefill(i, carry):
        first = jnp.maximum(i - (WINDOW - 1), 0)
        width = WINDOW * PLANE_ROWS
        keys = kvhome[0, pl.ds(first, WINDOW)].reshape(width, HD)
        values = kvhome[1, pl.ds(first, WINDOW)].reshape(width, HD)
        row_of = i * PLANE_ROWS + lax.broadcasted_iota(jnp.int32, (PLANE_ROWS, width), 0)
        spot = first * PLANE_ROWS + lax.broadcasted_iota(jnp.int32, (PLANE_ROWS, width), 1)
        begin_of = starts_of(row_of, home_lens)
        mask = jnp.where((spot >= begin_of) & (spot <= row_of), 0.0, neg_large)
        query = qhome[i].reshape(HEADS * PLANE_ROWS, HD)
        scores = scores_of(query, keys).reshape(HEADS, PLANE_ROWS, width) + mask[None]
        out = softmax_mix(scores.reshape(HEADS * PLANE_ROWS, width), values)
        rows_here = pl.ds(pl.multiple_of(i * PLANE_ROWS, PLANE_ROWS), PLANE_ROWS)
        for h in range(HEADS):
            prefill_ref[rows_here, h * HD : (h + 1) * HD] = out[
                h * PLANE_ROWS : (h + 1) * PLANE_ROWS
            ].astype(jnp.bfloat16)
        return carry

    lax.fori_loop(0, PLANES, prefill, 0)

    landed(dec.at[1 - y, new_cols], new_recv.at[0])
    for kind in range(2):
        for i in range(REPS):
            mine = (kind == core) & (i == rep) & (off)

            @pl.when(jnp.logical_not(mine))
            def _():
                landed(
                    dec.at[kind, pl.ds(i * PLANE_ROWS, PLANE_ROWS)], p2_recv.at[kind * PLANES + i]
                )

    for h in range(HEADS):
        scores = scores_of(queries_ref[:, h * HD : (h + 1) * HD], dec[0]) + bias[...]
        decode_ref[:, h * HD : (h + 1) * HD] = softmax_mix(scores, dec[1]).astype(jnp.bfloat16)

    landed(new_ref, new_send.at[0])
    for k in range(7):
        landed(block(0, 0), up_send.at[k])
        landed(block(0, 0), down_send.at[k])
    for k in range(16):
        landed(block(0, 0), sib_send.at[k])
    for slot in range(PLANES):
        landed(kvstage.at[0], kv_send.at[slot])

    @pl.when(off)
    def _():
        for h in range(2):
            landed(block(0, h), xs_send.at[h])
        landed(wq_low, w_send.at[0])
        landed(wq_high, w_send.at[1])
        landed(wkv, w_send.at[2])
        for slot in range(PLANES):
            landed(kvstage.at[0], kv_send2.at[slot])
            landed(qstage.at[0], q_send.at[slot])

    def drain(slot, carry):
        high = (z + slot // 2) % PLANES
        low = (z + 2 * PLANES - 1 - slot // 2) % PLANES
        plane = jnp.where(slot % 2 == 0, high, low)

        @pl.when(plane != rep)
        def _():
            landed(kvstage.at[0], p1_send.at[slot])

        for y2 in range(2):
            mine = (1 - y == core) & (slot == rep) & (y == y2)

            @pl.when(jnp.logical_not(mine))
            def _():
                landed(p2.at[0], p2_send.at[2 * slot + y2])

        return carry

    lax.fori_loop(0, PLANES, drain, 0)


def per_device(prompt_states, w_query, w_kv, queries, new_kv, lengths, pairing, assign, cache_len):
    depth = prompt_states.shape[-1]
    q_cols = w_query.shape[1]
    half = np.arange(HD // 2, dtype=np.float32) / np.float32(HD // 2)
    inverse = np.power(np.float32(theta_base), -half).astype(np.float32)
    freq = jnp.asarray(np.concatenate([inverse, inverse])[None, :])
    vmem = pl.BlockSpec(memory_space=pltpu.VMEM)
    smem = pl.BlockSpec(memory_space=pltpu.SMEM)
    anywhere = pl.BlockSpec(memory_space=pl.ANY)
    dma = pltpu.SemaphoreType.DMA
    bf16 = jnp.bfloat16
    prefill_out, decode_out = pl.pallas_call(
        kernel,
        out_shape=(
            jax.ShapeDtypeStruct((CACHE, q_cols), bf16),
            jax.ShapeDtypeStruct((NEW, q_cols), bf16),
        ),
        in_specs=[anywhere, anywhere, anywhere, vmem, vmem, smem, smem, vmem, vmem, vmem],
        out_specs=(vmem, vmem),
        scratch_shapes=[
            pltpu.VMEM((PLANES, PLANE_ROWS, depth), bf16),
            pltpu.VMEM((depth, q_cols), bf16),
            pltpu.VMEM((depth, HD), bf16),
            pltpu.VMEM((2 * PLANE_ROWS, q_cols + HD), jnp.float32),
            pltpu.VMEM((PLANES, PLANE_ROWS, HD), jnp.float32),
            pltpu.VMEM((PLANES, PLANE_ROWS, HD), jnp.float32),
            pltpu.VMEM((NEW, CACHE + NEW), jnp.float32),
            pltpu.VMEM((PLANES, HEADS, PLANE_ROWS, HD), bf16),
            pltpu.VMEM((PLANES, HEADS, PLANE_ROWS, HD), bf16),
            pltpu.VMEM((2, PLANES, PLANE_ROWS, HD), bf16),
            pltpu.VMEM((PLANES, PLANE_ROWS, HD), bf16),
            pltpu.VMEM((REPS, PLANE_ROWS, HD), bf16),
            pltpu.VMEM((REPS, PLANE_ROWS, HD), bf16),
            pltpu.VMEM((2, CACHE + NEW, HD), bf16),
            dma((2,)),
            dma((2,)),
            dma((3,)),
            dma((3,)),
            dma((7,)),
            dma((7,)),
            dma((7,)),
            dma((7,)),
            dma((16,)),
            dma((16,)),
            dma((1,)),
            dma((1,)),
            dma((PLANES,)),
            dma((PLANES,)),
            dma((PLANES,)),
            dma((PLANES,)),
            dma((2 * PLANES,)),
            dma((PLANES,)),
            dma((REPS,)),
            dma((2 * REPS,)),
            dma((2 * REPS,)),
        ],
        compiler_params=pltpu.CompilerParams(
            collective_id=0, has_side_effects=True, vmem_limit_bytes=56 * 1024 * 1024
        ),
        cost_estimate=pl.CostEstimate(
            flops=2 * CACHE * depth * (q_cols + HD) + 8 * CACHE * CACHE * q_cols,
            bytes_accessed=2 * depth * (q_cols + HD + TOK),
            transcendentals=2 * HEADS * CACHE * CACHE,
        ),
    )(
        prompt_states.reshape(TOK, depth),
        w_query,
        w_kv,
        queries.reshape(NEW, q_cols),
        new_kv.reshape(NEW, HD),
        lengths,
        pairing,
        assign.reshape(1, ROWS),
        cache_len.reshape(1, ROWS),
        freq,
    )
    return (
        prefill_out.reshape(1, 1, CACHE, q_cols),
        decode_out.reshape(1, 1, STEPS, ROWS, q_cols),
    )


def solution(mesh):
    placed = (
        P("pool", "rep", "tp", None),
        P(None, "tp"),
        P(None, "tp"),
        P("pool", "rep", None, None, "tp"),
        P("pool", "rep", None, None, "tp"),
        P(),
        P(),
        P("pool", "rep", None),
        P("pool", "rep", None),
    )
    return jax.shard_map(
        per_device,
        mesh=mesh,
        in_specs=placed,
        out_specs=(P("pool", "rep", None, "tp"), P("pool", "rep", None, None, "tp")),
        check_vma=False,
    )
```

```python
import functools
import math

import jax
import jax.numpy as jnp
import numpy as np
from jax import lax
from jax.experimental import pallas as pl
from jax.experimental.pallas import tpu as pltpu
from jax.sharding import PartitionSpec as P

HD = 128
PLANES = 8
REPS = 8
HEADS = 4
TOK = 64
PLANE_ROWS = 2 * TOK
WINDOW = 5
STEPS = 4
ROWS = 64
NEW = STEPS * ROWS
CACHE = PLANES * PLANE_ROWS
W_PIECE = 256
W_LOW_PIECES = 3
W_PIECES = 8
N_TILE = 256
WORK = HEADS * PLANE_ROWS

theta_base = 500000.0
neg_large = -1e30
exp_scale = math.log2(math.e) / math.sqrt(HD)


def remote(src, dst, send_sem, recv_sem, device):
    pltpu.make_async_remote_copy(
        src_ref=src,
        dst_ref=dst,
        send_sem=send_sem,
        recv_sem=recv_sem,
        device_id=device,
        device_id_type=pl.DeviceIdType.MESH,
    ).start()


def landed(ref, sem):
    pltpu.make_async_copy(ref, ref, sem).wait()


def scores_of(query, keys):
    return lax.dot_general(
        query, keys, (((1,), (1,)), ((), ())), preferred_element_type=jnp.float32
    )


def kernel(
    x_hbm,
    wq_hbm,
    wkv_hbm,
    queries_ref,
    new_ref,
    lengths_ref,
    pairing_ref,
    assign_ref,
    cache_len_ref,
    freq_ref,
    prefill_ref,
    decode_ref,
    xg,
    wall,
    accs,
    partial,
    cos_t,
    sin_t,
    bias,
    qhome,
    qstage,
    kvhome,
    kvstage,
    p1,
    p2,
    dec,
    top,
    total,
    mix,
    dec_top,
    dec_total,
    dec_mix,
    x0_sem,
    xs_send,
    wl_sem,
    wq_send,
    wq_recv,
    wkv_send,
    wkv_recv,
    wx_send,
    wx_recv,
    up_send,
    up_recv,
    down_send,
    down_recv,
    part_send,
    part_recv,
    new_send,
    new_recv,
    q_send,
    q_recv,
    kv_send,
    kv_send2,
    kv_recv,
    p1_send,
    p1_recv,
    p2_send,
    p2_recv,
):
    core = lax.axis_index("pool")
    rep = lax.axis_index("rep")
    t = lax.axis_index("tp")
    z = t // 2
    y = t % 2
    diag = core == y
    off = core != y
    other = 1 - core

    def dev(c2, g2, z2, y2):
        return (c2, g2, z2 * 2 + y2)

    up_dev = dev(core, rep, (z + 1) % PLANES, y)
    down_dev = dev(core, rep, (z + PLANES - 1) % PLANES, y)
    sibling = dev(other, rep, z, y)
    swap_low = dev(other, rep, z, 1 - y)
    across = dev(core, rep, z, 1 - y)
    across_high = dev(core, (rep + REPS // 2) % REPS, z, 1 - y)
    q_cols = wq_hbm.shape[1]
    parity = rep % 2
    row_of_x = rep // 4 * 4
    right = dev(core, row_of_x + (rep + 1) % 4, z, y)
    left = dev(core, row_of_x + (rep + 3) % 4, z, y)
    half_depth = W_PIECES * W_PIECE

    depth = wall.shape[0]
    cols = q_cols + HD
    own_depth = pl.multiple_of(core * depth, depth)
    other_depth = pl.multiple_of(other * depth, depth)
    mine_cols = pl.ds(pl.multiple_of(core * cols, HD), cols)
    sibling_cols = pl.ds(pl.multiple_of(other * cols, HD), cols)
    far_cols = pl.ds(pl.multiple_of((1 - y) * cols, HD), cols)
    far_q_cols = pl.ds(pl.multiple_of((1 - y) * cols, HD), q_cols)
    far_kv_cols = pl.ds(pl.multiple_of((1 - y) * cols + q_cols, HD), HD)
    near_q_cols = pl.ds(pl.multiple_of(y * cols, HD), q_cols)
    near_kv_cols = pl.ds(pl.multiple_of(y * cols + q_cols, HD), HD)
    half_depth = W_PIECES * W_PIECE

    def depth_rows(half, n):
        return pl.ds(pl.multiple_of(half * half_depth + n * W_PIECE, W_PIECE), W_PIECE)

    def source_rows(half, n):
        start = core * depth + half * half_depth + n * W_PIECE
        return pl.ds(pl.multiple_of(start, W_PIECE), W_PIECE)

    def distance(plane):
        away = (plane + PLANES - z) % PLANES
        return jnp.minimum(away, PLANES - away)

    y_rows = pl.ds(pl.multiple_of(y * TOK, TOK), TOK)
    far_rows = pl.ds(pl.multiple_of((1 - y) * TOK, TOK), TOK)

    def block(slot, h):
        return xg.at[slot, y_rows if h == 0 else far_rows]

    @pl.when(diag)
    def _():
        pltpu.make_async_copy(
            x_hbm.at[:, pl.ds(own_depth, depth)], xg.at[0, y_rows], x0_sem.at[0]
        ).start()

    pltpu.make_async_copy(
        wq_hbm.at[pl.ds(own_depth, depth)], wall.at[:, near_q_cols], wl_sem.at[0]
    ).start()
    pltpu.make_async_copy(
        wkv_hbm.at[pl.ds(own_depth, depth)], wall.at[:, near_kv_cols], wl_sem.at[1]
    ).start()

    barrier = pltpu.get_barrier_semaphore()

    def greet(n, carry):
        c2 = n // 16
        g2 = (n // 2) % 8
        y2 = n % 2
        mine = (c2 == core) & (g2 == rep) & (y2 == y)

        @pl.when(jnp.logical_not(mine))
        def _():
            pl.semaphore_signal(
                barrier, inc=1, device_id=dev(c2, g2, z, y2), device_id_type=pl.DeviceIdType.MESH
            )

        return carry

    lax.fori_loop(0, 32, greet, 0)
    for device in (up_dev, down_dev):
        pl.semaphore_signal(
            barrier, inc=1, device_id=device, device_id_type=pl.DeviceIdType.MESH
        )
    pl.semaphore_wait(barrier, 33)

    @pl.when(diag)
    def _():
        remote(
            x_hbm.at[:, pl.ds(other_depth, depth)],
            xg.at[0, y_rows],
            xs_send.at[0],
            x0_sem.at[0],
            sibling,
        )

    @pl.when(off)
    def _():
        remote(
            x_hbm.at[:, pl.ds(own_depth, depth)],
            xg.at[0, y_rows],
            xs_send.at[0],
            x0_sem.at[1],
            across,
        )
        remote(
            x_hbm.at[:, pl.ds(other_depth, depth)],
            xg.at[0, y_rows],
            xs_send.at[1],
            x0_sem.at[1],
            swap_low,
        )

    for n in range(W_PIECES):
        target = across if n < W_LOW_PIECES else across_high
        remote(
            wq_hbm.at[source_rows(parity, n)],
            wall.at[depth_rows(parity, n), near_q_cols],
            wq_send.at[n],
            wq_recv.at[n],
            target,
        )
        remote(
            wkv_hbm.at[source_rows(parity, n)],
            wall.at[depth_rows(parity, n), near_kv_cols],
            wkv_send.at[n],
            wkv_recv.at[n],
            target,
        )

    def pass_on(pieces):
        for n in pieces:
            rows = depth_rows(parity, n)
            landed(wall.at[rows, far_q_cols], wq_recv.at[n])
            landed(wall.at[rows, far_kv_cols], wkv_recv.at[n])
            target = right if n < W_LOW_PIECES else left
            piece = wall.at[rows, far_cols]
            remote(piece, piece, wx_send.at[n], wx_recv.at[n], target)

    def send_up(src, dst, h, k):
        remote(block(src, h), block(dst, h), up_send.at[k], up_recv.at[k], up_dev)

    def send_down(src, dst, h, k):
        remote(block(src, h), block(dst, h), down_send.at[k], down_recv.at[k], down_dev)

    for h in range(2):
        landed(block(0, h), x0_sem.at[h])
        send_up(0, 1, h, h)
        send_down(0, 2, h, h)

    new_cols = pl.ds(CACHE, NEW)
    remote(new_ref, dec.at[y, new_cols], new_send.at[0], new_recv.at[0], across)
    dec[y, new_cols] = new_ref[...]

    def starts_of(rows, lens):
        end = jnp.int32(0)
        total = jnp.zeros_like(rows)
        for length in lens:
            end = end + length
            total = total + jnp.where(rows >= end, length, 0)
        return total

    work_lens = [lengths_ref[y, j, rep] for j in range(4)]
    home_lens = [lengths_ref[core, j, rep] for j in range(4)]
    paired = pairing_ref[core, rep]
    pair_lens = [lengths_ref[other, j, paired] for j in range(4)]

    def tables(plane, carry):
        rows = plane * PLANE_ROWS + lax.broadcasted_iota(jnp.int32, (PLANE_ROWS, HD), 0)
        lanes = lax.broadcasted_iota(jnp.int32, (PLANE_ROWS, HD), 1)
        offset = (rows - starts_of(rows, work_lens)).astype(jnp.float32)
        angle = offset * freq_ref[...]
        cos_t[plane] = jnp.cos(angle)
        sine = jnp.sin(angle)
        sin_t[plane] = jnp.where(lanes < HD // 2, -sine, sine)
        return carry

    lax.fori_loop(0, PLANES, tables, 0)

    def column(ref):
        spread = jnp.broadcast_to(ref[...], (ROWS, ROWS))
        here = lax.broadcasted_iota(jnp.int32, (ROWS, ROWS), 0) == lax.broadcasted_iota(
            jnp.int32, (ROWS, ROWS), 1
        )
        picked = jnp.where(here, spread.astype(jnp.float32), 0.0)
        return jnp.sum(picked, axis=1, keepdims=True).astype(jnp.int32)

    member = column(assign_ref)
    limit = column(cache_len_ref)
    lower = jnp.zeros_like(member)
    extent = jnp.zeros_like(member)
    begin = jnp.int32(0)
    for j in range(4):
        lower = jnp.where(member == j, begin, lower)
        extent = jnp.where(member == j, pair_lens[j], extent)
        begin = begin + pair_lens[j]
    upper = lower + jnp.minimum(extent, limit)
    spots = lax.broadcasted_iota(jnp.int32, (ROWS, CACHE), 1)
    visible = jnp.where((spots >= lower) & (spots < upper), 0.0, neg_large)
    new_spot = lax.broadcasted_iota(jnp.int32, (ROWS, NEW), 1)
    row = lax.broadcasted_iota(jnp.int32, (ROWS, NEW), 0)
    for s in range(STEPS):
        rows_here = pl.ds(s * ROWS, ROWS)
        bias[rows_here, pl.ds(0, CACHE)] = visible
        own = (new_spot % ROWS == row) & (new_spot // ROWS <= s)
        bias[rows_here, new_cols] = jnp.where(own, 0.0, neg_large)

    def relay(d, h):
        k = 2 * (d - 1) + h
        low, high = 2 * d - 1, 2 * d
        landed(block(low, h), up_recv.at[k])
        if d < 3:
            send_up(low, low + 2, h, k + 2)
        elif h == 0:
            send_up(low, low + 2, h, 6)
        landed(block(high, h), down_recv.at[k])
        if d < 3:
            send_down(high, high + 2, h, k + 2)
        elif h == 1:
            send_down(high, 7, h, 6)

    def finish_plane(slot, plane, rows):
        cosine = cos_t[plane]
        sine = sin_t[plane]

        def turned(part):
            return part * cosine + pltpu.roll(part, HD // 2, 1) * sine

        heads = [turned(rows[:, h * HD : (h + 1) * HD]).astype(jnp.bfloat16) for h in range(HEADS)]
        raw = rows[:, HEADS * HD :]
        own = jnp.where(core == 0, turned(raw), raw).astype(jnp.bfloat16)
        kvstage[plane] = own

        @pl.when(diag)
        def _():
            for h in range(HEADS):
                qhome[plane, h] = heads[h]
            kvhome[core, plane] = own
            remote(
                kvstage.at[plane],
                kvhome.at[core, plane],
                kv_send.at[slot],
                kv_recv.at[core * PLANES + plane],
                across,
            )

        @pl.when(off)
        def _():
            for h in range(HEADS):
                qstage[slot, h] = heads[h]
            remote(
                kvstage.at[plane],
                kvhome.at[core, plane],
                kv_send.at[slot],
                kv_recv.at[core * PLANES + plane],
                swap_low,
            )
            remote(
                kvstage.at[plane],
                kvhome.at[core, plane],
                kv_send2.at[slot],
                kv_recv.at[core * PLANES + plane],
                sibling,
            )
            remote(qstage.at[slot], qhome.at[plane], q_send.at[slot], q_recv.at[plane], swap_low)

        @pl.when(plane == rep)
        def _():
            p1[rep] = own

        @pl.when(plane != rep)
        def _():
            remote(
                kvstage.at[plane],
                p1.at[rep],
                p1_send.at[slot],
                p1_recv.at[rep],
                dev(core, plane, z, y),
            )

    def project(first, count):
        rows_here = count * PLANE_ROWS

        def tile(n, carry):
            wide = pl.ds(pl.multiple_of(n * N_TILE, N_TILE), N_TILE)
            rows = xg[pl.ds(first, count)].reshape(rows_here, depth)
            out = jnp.dot(rows, wall[:, wide], preferred_element_type=jnp.float32)
            accs[pl.ds(first, count), :, wide] = out.reshape(count, PLANE_ROWS, N_TILE)
            return carry

        lax.fori_loop(0, wall.shape[1] // N_TILE, tile, 0)
        for slot in range(first, first + count):
            remote(
                accs.at[slot, :, sibling_cols],
                partial.at[slot],
                part_send.at[slot],
                part_recv.at[slot],
                sibling,
            )

    def finish(slots):
        for slot, away in slots:
            landed(partial.at[slot], part_recv.at[slot])
            rows = accs[slot, :, mine_cols] + partial[slot]
            finish_plane(slot, (z + PLANES + away) % PLANES, rows)

    cache_rows = pl.ds(pl.multiple_of(rep * PLANE_ROWS, PLANE_ROWS), PLANE_ROWS)

    def hand_over(nearest, farthest):
        here = distance(rep)

        @pl.when((here >= nearest) & (here <= farthest))
        def _():
            for g2 in range(REPS):

                @pl.when(rep != g2)
                def _():
                    landed(p1.at[g2], p1_recv.at[g2])

            def give(d, carry):
                p2[d] = p1[pairing_ref[1 - y, d]]
                for y2 in range(2):
                    mine = (1 - y == core) & (d == rep) & (y == y2)

                    @pl.when(mine)
                    def _():
                        dec[core, cache_rows] = p2[d]

                    @pl.when(jnp.logical_not(mine))
                    def _():
                        remote(
                            p2.at[d],
                            dec.at[core, cache_rows],
                            p2_send.at[2 * d + y2],
                            p2_recv.at[core * PLANES + rep],
                            dev(1 - y, d, z, y2),
                        )

                return carry

            lax.fori_loop(0, REPS, give, 0)

    def home_landed(away):
        plane = (z + PLANES + away) % PLANES

        @pl.when(off)
        def _():
            landed(qhome.at[plane], q_recv.at[plane])
            landed(kvhome.at[0, plane], kv_recv.at[plane])
            landed(kvhome.at[1, plane], kv_recv.at[PLANES + plane])

        @pl.when(diag)
        def _():
            landed(kvhome.at[other, plane], kv_recv.at[other * PLANES + plane])

    def attend(i, planes, fresh):
        width = len(planes) * PLANE_ROWS
        row_of = i * PLANE_ROWS + lax.broadcasted_iota(jnp.int32, (PLANE_ROWS, 1), 0)
        lanes = lax.broadcasted_iota(jnp.int32, (PLANE_ROWS, PLANE_ROWS), 1)
        spot = jnp.concatenate([lanes + j * PLANE_ROWS for j in planes], axis=1)
        keys = jnp.concatenate([kvhome[0, j] for j in planes], axis=0)
        values = jnp.concatenate([kvhome[1, j] for j in planes], axis=0)
        begin_of = starts_of(row_of, home_lens)
        mask = jnp.where((spot >= begin_of) & (spot <= row_of), 0.0, neg_large)
        scores = scores_of(qhome[i].reshape(WORK, HD), keys)
        scores = (scores.reshape(HEADS, PLANE_ROWS, width) + mask[None]).reshape(WORK, width)
        peak = jnp.max(scores, axis=-1, keepdims=True)
        if not fresh:
            before = top[i]
            peak = jnp.maximum(before[:, :1], peak)
            fade = jnp.exp2((before - peak) * exp_scale)
        weights = jnp.exp2((scores - peak) * exp_scale)
        summed = jnp.sum(weights, axis=-1, keepdims=True)
        mixed = jnp.dot(weights.astype(jnp.bfloat16), values, preferred_element_type=jnp.float32)
        if fresh:
            total[i] = jnp.broadcast_to(summed, (WORK, HD))
            mix[i] = mixed
        else:
            total[i] = total[i] * fade + summed
            mix[i] = mix[i] * fade + mixed
        top[i] = jnp.broadcast_to(peak, (WORK, HD))

    def plane_at(away):
        return (z + PLANES + away) % PLANES

    def attend_near():
        planes = [plane_at(away) for away in near]

        def one(n, carry):
            attend((z + PLANES - 2 + n) % PLANES, planes, True)
            return carry

        lax.fori_loop(0, 5, one, 0)

    def attend_third():
        planes = [plane_at(-3), plane_at(3)]

        def one(n, carry):
            attend((z + PLANES - 2 + n) % PLANES, planes, False)
            return carry

        lax.fori_loop(0, 5, one, 0)

        def two(n, carry):
            attend((z + PLANES - 3 + 6 * n) % PLANES, planes + [plane_at(a) for a in near], True)
            return carry

        lax.fori_loop(0, 2, two, 0)

    def attend_last():
        last = plane_at(4)
        first = jnp.maximum(last - (WINDOW - 1), 0)
        attend(last, [first + n for n in range(WINDOW)], True)

        def one(n, carry):
            i = last + 1 + n

            @pl.when(i < PLANES)
            def _():
                attend(i, [last], False)

            return carry

        lax.fori_loop(0, WINDOW - 1, one, 0)

    def settle(late):
        def one(i, carry):
            after = i - (z + 4) % PLANES
            needs_last = (after >= 0) & (after < WINDOW)

            @pl.when(needs_last if late else jnp.logical_not(needs_last))
            def _():
                out = mix[i] / total[i]
                rows_here = pl.ds(pl.multiple_of(i * PLANE_ROWS, PLANE_ROWS), PLANE_ROWS)
                for h in range(HEADS):
                    prefill_ref[rows_here, h * HD : (h + 1) * HD] = out[
                        h * PLANE_ROWS : (h + 1) * PLANE_ROWS
                    ].astype(jnp.bfloat16)

            return carry

        lax.fori_loop(0, PLANES, one, 0)

    def caches_landed(aways):
        for away in aways:
            plane = (z + PLANES + away) % PLANES
            rows_here = pl.ds(pl.multiple_of(plane * PLANE_ROWS, PLANE_ROWS), PLANE_ROWS)
            for kind in range(2):
                mine = (kind == core) & (plane == rep) & off

                @pl.when(jnp.logical_not(mine))
                def _():
                    landed(dec.at[kind, rows_here], p2_recv.at[kind * PLANES + plane])

    def cache_slices(aways):
        slices = []
        for away in aways:
            plane = (z + PLANES + away) % PLANES
            slices.append(pl.ds(pl.multiple_of(plane * PLANE_ROWS, PLANE_ROWS), PLANE_ROWS))
        return slices

    def decode_scores(h, slices):
        query = queries_ref[:, h * HD : (h + 1) * HD]
        keys = jnp.concatenate([dec[0, piece] for piece in slices], axis=0)
        mask = jnp.concatenate([bias[:, piece] for piece in slices], axis=1)
        values = jnp.concatenate([dec[1, piece] for piece in slices], axis=0)
        return scores_of(query, keys) + mask, values

    def decode_first(aways):
        slices = cache_slices(aways) + [new_cols]
        for h in range(HEADS):
            scores, values = decode_scores(h, slices)
            peak = jnp.max(scores, axis=-1, keepdims=True)
            weights = jnp.exp2((scores - peak) * exp_scale)
            dec_top[h] = jnp.broadcast_to(peak, (NEW, HD))
            dec_total[h] = jnp.broadcast_to(
                jnp.sum(weights, axis=-1, keepdims=True), (NEW, HD)
            )
            dec_mix[h] = jnp.dot(
                weights.astype(jnp.bfloat16), values, preferred_element_type=jnp.float32
            )

    def decode_last(aways):
        slices = cache_slices(aways)
        for h in range(HEADS):
            scores, values = decode_scores(h, slices)
            before = dec_top[h]
            peak = jnp.maximum(before, jnp.max(scores, axis=-1, keepdims=True))
            fade = jnp.exp2((before - peak) * exp_scale)
            weights = jnp.exp2((scores - peak[:, :1]) * exp_scale)
            whole = dec_total[h] * fade + jnp.sum(weights, axis=-1, keepdims=True)
            mixed = dec_mix[h] * fade + jnp.dot(
                weights.astype(jnp.bfloat16), values, preferred_element_type=jnp.float32
            )
            decode_ref[:, h * HD : (h + 1) * HD] = (mixed / whole).astype(jnp.bfloat16)

    near = (0, -1, 1, -2, 2)
    relay(1, 0)
    pass_on((3, 4))
    relay(1, 1)
    pass_on((0, 5, 1, 6))
    relay(2, 0)
    pass_on((2, 7))
    relay(2, 1)
    landed(wall.at[:, near_q_cols], wl_sem.at[0])
    landed(wall.at[:, near_kv_cols], wl_sem.at[1])
    for n in range(W_PIECES):
        landed(wall.at[depth_rows(1 - parity, n), far_cols], wx_recv.at[n])

    project(0, 5)
    relay(3, 0)
    finish(((0, 0), (1, -1), (2, 1), (3, -2), (4, 2)))
    hand_over(0, 2)
    for away in near:
        home_landed(away)
    attend_near()
    relay(3, 1)
    project(5, 2)
    landed(dec.at[1 - y, new_cols], new_recv.at[0])
    caches_landed(near)
    decode_first(near)
    finish(((5, -3), (6, 3)))
    hand_over(3, 3)
    for away in (-3, 3):
        home_landed(away)
    attend_third()
    settle(False)
    landed(block(7, 0), up_recv.at[6])
    landed(block(7, 1), down_recv.at[6])
    project(7, 1)
    finish(((7, 4),))
    hand_over(4, 4)
    home_landed(4)
    attend_last()
    settle(True)
    far = (-3, 3, 4)
    caches_landed(far)
    decode_last(far)

    landed(new_ref, new_send.at[0])
    for k in range(7):
        landed(block(0, 0), up_send.at[k])
        landed(block(0, 0), down_send.at[k])
    landed(block(0, 0), xs_send.at[0])
    for slot in range(PLANES):
        landed(kvstage.at[0], kv_send.at[slot])
        landed(partial.at[0], part_send.at[slot])
    for n in range(W_PIECES):
        rows = depth_rows(0, n)
        landed(wall.at[rows, near_q_cols], wq_send.at[n])
        landed(wall.at[rows, near_kv_cols], wkv_send.at[n])
        landed(wall.at[rows, far_cols], wx_send.at[n])

    @pl.when(off)
    def _():
        landed(block(0, 0), xs_send.at[1])
        for slot in range(PLANES):
            landed(kvstage.at[0], kv_send2.at[slot])
            landed(qstage.at[0], q_send.at[slot])

    def drain(slot, carry):
        odd = slot % 2
        step = (slot + odd) // 2
        plane = jnp.where(odd == 0, (z + step) % PLANES, (z + PLANES - step) % PLANES)

        @pl.when(plane != rep)
        def _():
            landed(kvstage.at[0], p1_send.at[slot])

        for y2 in range(2):
            mine = (1 - y == core) & (slot == rep) & (y == y2)

            @pl.when(jnp.logical_not(mine))
            def _():
                landed(p2.at[0], p2_send.at[2 * slot + y2])

        return carry

    lax.fori_loop(0, PLANES, drain, 0)


def per_device(prompt_states, w_query, w_kv, queries, new_kv, lengths, pairing, assign, cache_len):
    depth = prompt_states.shape[-1]
    q_cols = w_query.shape[1]
    half = np.arange(HD // 2, dtype=np.float32) / np.float32(HD // 2)
    inverse = np.power(np.float32(theta_base), -half).astype(np.float32)
    freq = jnp.asarray(np.concatenate([inverse, inverse])[None, :])
    vmem = pl.BlockSpec(memory_space=pltpu.VMEM)
    smem = pl.BlockSpec(memory_space=pltpu.SMEM)
    anywhere = pl.BlockSpec(memory_space=pl.ANY)
    dma = pltpu.SemaphoreType.DMA
    bf16 = jnp.bfloat16
    prefill_out, decode_out = pl.pallas_call(
        kernel,
        out_shape=(
            jax.ShapeDtypeStruct((CACHE, q_cols), bf16),
            jax.ShapeDtypeStruct((NEW, q_cols), bf16),
        ),
        in_specs=[anywhere, anywhere, anywhere, vmem, vmem, smem, smem, vmem, vmem, vmem],
        out_specs=(vmem, vmem),
        scratch_shapes=[
            pltpu.VMEM((PLANES, PLANE_ROWS, depth // 2), bf16),
            pltpu.VMEM((depth // 2, 2 * (q_cols + HD)), bf16),
            pltpu.VMEM((PLANES, PLANE_ROWS, 2 * (q_cols + HD)), jnp.float32),
            pltpu.VMEM((PLANES, PLANE_ROWS, q_cols + HD), jnp.float32),
            pltpu.VMEM((PLANES, PLANE_ROWS, HD), jnp.float32),
            pltpu.VMEM((PLANES, PLANE_ROWS, HD), jnp.float32),
            pltpu.VMEM((NEW, CACHE + NEW), jnp.float32),
            pltpu.VMEM((PLANES, HEADS, PLANE_ROWS, HD), bf16),
            pltpu.VMEM((PLANES, HEADS, PLANE_ROWS, HD), bf16),
            pltpu.VMEM((2, PLANES, PLANE_ROWS, HD), bf16),
            pltpu.VMEM((PLANES, PLANE_ROWS, HD), bf16),
            pltpu.VMEM((REPS, PLANE_ROWS, HD), bf16),
            pltpu.VMEM((REPS, PLANE_ROWS, HD), bf16),
            pltpu.VMEM((2, CACHE + NEW, HD), bf16),
            pltpu.VMEM((PLANES, WORK, HD), jnp.float32),
            pltpu.VMEM((PLANES, WORK, HD), jnp.float32),
            pltpu.VMEM((PLANES, WORK, HD), jnp.float32),
            pltpu.VMEM((HEADS, NEW, HD), jnp.float32),
            pltpu.VMEM((HEADS, NEW, HD), jnp.float32),
            pltpu.VMEM((HEADS, NEW, HD), jnp.float32),
            dma((2,)),
            dma((2,)),
            dma((2,)),
            dma((W_PIECES,)),
            dma((W_PIECES,)),
            dma((W_PIECES,)),
            dma((W_PIECES,)),
            dma((W_PIECES,)),
            dma((W_PIECES,)),
            dma((7,)),
            dma((7,)),
            dma((7,)),
            dma((7,)),
            dma((PLANES,)),
            dma((PLANES,)),
            dma((1,)),
            dma((1,)),
            dma((PLANES,)),
            dma((PLANES,)),
            dma((PLANES,)),
            dma((PLANES,)),
            dma((2 * PLANES,)),
            dma((PLANES,)),
            dma((REPS,)),
            dma((2 * REPS,)),
            dma((2 * REPS,)),
        ],
        compiler_params=pltpu.CompilerParams(
            collective_id=0, has_side_effects=True, vmem_limit_bytes=56 * 1024 * 1024
        ),
        cost_estimate=pl.CostEstimate(
            flops=2 * CACHE * depth * (q_cols + HD) + 8 * CACHE * CACHE * q_cols,
            bytes_accessed=2 * depth * (q_cols + HD + TOK),
            transcendentals=2 * HEADS * CACHE * CACHE,
        ),
    )(
        prompt_states.reshape(TOK, depth),
        w_query,
        w_kv,
        queries.reshape(NEW, q_cols),
        new_kv.reshape(NEW, HD),
        lengths.transpose(0, 2, 1),
        pairing,
        assign.reshape(1, ROWS),
        cache_len.reshape(1, ROWS),
        freq,
    )
    return (
        prefill_out.reshape(1, 1, CACHE, q_cols),
        decode_out.reshape(1, 1, STEPS, ROWS, q_cols),
    )


def solution(mesh):
    placed = (
        P("pool", "rep", "tp", None),
        P(None, "tp"),
        P(None, "tp"),
        P("pool", "rep", None, None, "tp"),
        P("pool", "rep", None, None, "tp"),
        P(),
        P(),
        P("pool", "rep", None),
        P("pool", "rep", None),
    )
    return jax.shard_map(
        per_device,
        mesh=mesh,
        in_specs=placed,
        out_specs=(P("pool", "rep", None, "tp"), P("pool", "rep", None, None, "tp")),
        check_vma=False,
    )
```

```python
import functools
import math

import jax
import jax.numpy as jnp
import numpy as np
from jax import lax
from jax.experimental import pallas as pl
from jax.experimental.pallas import tpu as pltpu
from jax.sharding import PartitionSpec as P

HD = 128
PLANES = 8
REPS = 8
HEADS = 4
TOK = 64
HALF = 32
PLANE_ROWS = 2 * TOK
WINDOW = 5
STEPS = 4
ROWS = 64
NEW = STEPS * ROWS
CACHE = PLANES * PLANE_ROWS
W_LOW = 2560
K_CHUNK = 2048

theta_base = 500000.0
neg_large = -1e30
exp_scale = math.log2(math.e) / math.sqrt(HD)


def remote(src, dst, send_sem, recv_sem, device):
    pltpu.make_async_remote_copy(
        src_ref=src,
        dst_ref=dst,
        send_sem=send_sem,
        recv_sem=recv_sem,
        device_id=device,
        device_id_type=pl.DeviceIdType.MESH,
    ).start()


def landed(ref, sem):
    pltpu.make_async_copy(ref, ref, sem).wait()


def softmax_mix(scores, values):
    peak = jnp.max(scores, axis=-1, keepdims=True)
    weights = jnp.exp2((scores - peak) * exp_scale)
    total = jnp.sum(weights, axis=-1, keepdims=True)
    mixed = jnp.dot(weights.astype(jnp.bfloat16), values, preferred_element_type=jnp.float32)
    return mixed / total


def starts_of(rows, lens):
    end = jnp.int32(0)
    total = jnp.zeros_like(rows)
    for length in lens:
        end = end + length
        total = total + jnp.where(rows >= end, length, 0)
    return total


def scores_of(query, keys):
    return lax.dot_general(
        query, keys, (((1,), (1,)), ((), ())), preferred_element_type=jnp.float32
    )


def kernel(
    x_hbm,
    wq_hbm,
    wkv_hbm,
    new_ref,
    lengths_ref,
    pairing_ref,
    freq_ref,
    q_out,
    kv_out,
    dec_out,
    xg,
    wq,
    wkv,
    acc,
    cos_t,
    sin_t,
    qhome,
    qstage,
    kvhome,
    kvstage,
    p1,
    p2,
    dec,
    x0_sem,
    xs_send,
    w_sem,
    w_send,
    up_send,
    up_recv,
    down_send,
    down_recv,
    sib_send,
    sib_recv,
    new_send,
    new_recv,
    q_send,
    q_recv,
    kv_send,
    kv_send2,
    kv_recv,
    p1_send,
    p1_recv,
    p2_send,
    p2_recv,
    out_sem,
):
    core = lax.axis_index("pool")
    rep = lax.axis_index("rep")
    t = lax.axis_index("tp")
    z = t // 2
    y = t % 2
    diag = core == y
    off = core != y
    other = 1 - core

    def dev(c2, g2, z2, y2):
        return (c2, g2, z2 * 2 + y2)

    up_dev = dev(core, rep, (z + 1) % PLANES, y)
    down_dev = dev(core, rep, (z + PLANES - 1) % PLANES, y)
    sibling = dev(other, rep, z, y)
    swap_low = dev(other, rep, z, 1 - y)
    swap_high = dev(other, (rep + REPS // 2) % REPS, z, 1 - y)
    across = dev(core, rep, z, 1 - y)
    row0 = pl.multiple_of(core * TOK, TOK)
    other_row0 = pl.multiple_of(other * TOK, TOK)

    wq_low = wq.at[pl.ds(0, W_LOW)]
    wq_high = wq.at[pl.ds(W_LOW, wq.shape[0] - W_LOW)]
    wq_hbm_low = wq_hbm.at[pl.ds(0, W_LOW)]
    wq_hbm_high = wq_hbm.at[pl.ds(W_LOW, wq.shape[0] - W_LOW)]

    def block(slot, half):
        return xg.at[slot, pl.ds(pl.multiple_of(row0 + half * HALF, HALF), HALF)]

    def sibling_block(slot, half):
        return xg.at[slot, pl.ds(pl.multiple_of(other_row0 + half * HALF, HALF), HALF)]

    @pl.when(diag)
    def _():
        for h in range(2):
            pltpu.make_async_copy(
                x_hbm.at[pl.ds(h * HALF, HALF)], block(0, h), x0_sem.at[h]
            ).start()
        pltpu.make_async_copy(wq_hbm_low, wq_low, w_sem.at[0]).start()
        pltpu.make_async_copy(wq_hbm_high, wq_high, w_sem.at[1]).start()
        pltpu.make_async_copy(wkv_hbm, wkv, w_sem.at[2]).start()

    barrier = pltpu.get_barrier_semaphore()

    def greet(n, carry):
        c2 = n // 16
        g2 = (n // 2) % 8
        y2 = n % 2
        mine = (c2 == core) & (g2 == rep) & (y2 == y)

        @pl.when(jnp.logical_not(mine))
        def _():
            pl.semaphore_signal(
                barrier, inc=1, device_id=dev(c2, g2, z, y2), device_id_type=pl.DeviceIdType.MESH
            )

        return carry

    lax.fori_loop(0, 32, greet, 0)
    for device in (up_dev, down_dev):
        pl.semaphore_signal(
            barrier, inc=1, device_id=device, device_id_type=pl.DeviceIdType.MESH
        )
    pl.semaphore_wait(barrier, 33)

    @pl.when(off)
    def _():
        for h in range(2):
            remote(
                x_hbm.at[pl.ds(h * HALF, HALF)],
                sibling_block(0, h),
                xs_send.at[h],
                x0_sem.at[h],
                swap_low,
            )
        remote(wq_hbm_high, wq_high, w_send.at[1], w_sem.at[1], swap_high)
        remote(wq_hbm_low, wq_low, w_send.at[0], w_sem.at[0], swap_low)
        remote(wkv_hbm, wkv, w_send.at[2], w_sem.at[2], swap_low)

    def send_up(src, dst, h, k):
        remote(block(src, h), block(dst, h), up_send.at[k], up_recv.at[k], up_dev)

    def send_down(src, dst, h, k):
        remote(block(src, h), block(dst, h), down_send.at[k], down_recv.at[k], down_dev)

    def share(slot, h):
        k = slot * 2 + h
        remote(block(slot, h), block(slot, h), sib_send.at[k], sib_recv.at[k], sibling)

    for h in range(2):
        landed(block(0, h), x0_sem.at[h])
        send_up(0, 1, h, h)
        send_down(0, 2, h, h)
        share(0, h)

    new_cols = pl.ds(CACHE, NEW)
    remote(new_ref, dec.at[y, new_cols], new_send.at[0], new_recv.at[0], across)
    dec[y, new_cols] = new_ref[...]

    work_lens = [lengths_ref[y, j, rep] for j in range(4)]

    def tables(plane, carry):
        rows = plane * PLANE_ROWS + lax.broadcasted_iota(jnp.int32, (PLANE_ROWS, HD), 0)
        lanes = lax.broadcasted_iota(jnp.int32, (PLANE_ROWS, HD), 1)
        offset = (rows - starts_of(rows, work_lens)).astype(jnp.float32)
        angle = offset * freq_ref[...]
        cos_t[plane] = jnp.cos(angle)
        sine = jnp.sin(angle)
        sin_t[plane] = jnp.where(lanes < HD // 2, -sine, sine)
        return carry

    lax.fori_loop(0, PLANES, tables, 0)

    def relay(d, h):
        k = 2 * (d - 1) + h
        low, high = 2 * d - 1, 2 * d
        landed(block(low, h), up_recv.at[k])
        if d < 3:
            send_up(low, low + 2, h, k + 2)
        elif h == 0:
            send_up(low, low + 2, h, 6)
        share(low, h)
        landed(block(high, h), down_recv.at[k])
        if d < 3:
            send_down(high, high + 2, h, k + 2)
        elif h == 1:
            send_down(high, 7, h, 6)
        share(high, h)

    for d in (1, 2):
        for h in range(2):
            relay(d, h)
    relay(3, 0)
    relay(3, 1)
    landed(wq_low, w_sem.at[0])
    landed(wq_high, w_sem.at[1])
    landed(wkv, w_sem.at[2])

    def finish_plane(slot, plane, rows):
        cosine = cos_t[plane]
        sine = sin_t[plane]

        def turned(part):
            return part * cosine + pltpu.roll(part, HD // 2, 1) * sine

        heads = [turned(rows[:, h * HD : (h + 1) * HD]).astype(jnp.bfloat16) for h in range(HEADS)]
        raw = rows[:, HEADS * HD :]
        own = jnp.where(core == 0, turned(raw), raw).astype(jnp.bfloat16)
        kvstage[plane] = own

        @pl.when(diag)
        def _():
            for h in range(HEADS):
                qhome[plane, h] = heads[h]
            kvhome[core, plane] = own
            remote(
                kvstage.at[plane],
                kvhome.at[core, plane],
                kv_send.at[slot],
                kv_recv.at[core * PLANES + plane],
                across,
            )

        @pl.when(off)
        def _():
            for h in range(HEADS):
                qstage[slot, h] = heads[h]
            remote(
                kvstage.at[plane],
                kvhome.at[core, plane],
                kv_send.at[slot],
                kv_recv.at[core * PLANES + plane],
                swap_low,
            )
            remote(
                kvstage.at[plane],
                kvhome.at[core, plane],
                kv_send2.at[slot],
                kv_recv.at[core * PLANES + plane],
                sibling,
            )
            remote(qstage.at[slot], qhome.at[plane], q_send.at[slot], q_recv.at[plane], swap_low)

        @pl.when(plane == rep)
        def _():
            p1[rep] = own

        @pl.when(plane != rep)
        def _():
            remote(
                kvstage.at[plane],
                p1.at[rep],
                p1_send.at[slot],
                p1_recv.at[rep],
                dev(core, plane, z, y),
            )

    def project(b, carry):
        @pl.when(b == 3)
        def _():
            landed(block(7, 0), up_recv.at[6])
            share(7, 0)
            landed(block(7, 1), down_recv.at[6])
            share(7, 1)

        for j in range(2):
            for h in range(2):
                landed(sibling_block(2 * b + j, h), sib_recv.at[4 * b + 2 * j + h])

        acc[...] = jnp.zeros_like(acc)

        def step(k, inner):
            deep = pl.ds(pl.multiple_of(k * K_CHUNK, K_CHUNK), K_CHUNK)
            rows = xg[pl.ds(2 * b, 2), :, deep].reshape(2 * PLANE_ROWS, K_CHUNK)
            acc[:, : HEADS * HD] += jnp.dot(
                rows, wq[deep, :], preferred_element_type=jnp.float32
            )
            acc[:, HEADS * HD :] += jnp.dot(
                rows, wkv[deep, :], preferred_element_type=jnp.float32
            )
            return inner

        lax.fori_loop(0, wq.shape[0] // K_CHUNK, step, 0)
        finish_plane(2 * b, (z + b) % PLANES, acc[pl.ds(0, PLANE_ROWS), :])
        finish_plane(
            2 * b + 1, (z + 2 * PLANES - 1 - b) % PLANES, acc[pl.ds(PLANE_ROWS, PLANE_ROWS), :]
        )
        return carry

    lax.fori_loop(0, PLANES // 2, project, 0)

    for g2 in range(REPS):

        @pl.when(rep != g2)
        def _():
            landed(p1.at[g2], p1_recv.at[g2])

    cache_rows = pl.ds(pl.multiple_of(rep * PLANE_ROWS, PLANE_ROWS), PLANE_ROWS)

    def hand_over(d, carry):
        p2[d] = p1[pairing_ref[1 - y, d]]
        for y2 in range(2):
            mine = (1 - y == core) & (d == rep) & (y == y2)

            @pl.when(mine)
            def _():
                dec[core, cache_rows] = p2[d]

            @pl.when(jnp.logical_not(mine))
            def _():
                remote(
                    p2.at[d],
                    dec.at[core, cache_rows],
                    p2_send.at[2 * d + y2],
                    p2_recv.at[core * PLANES + rep],
                    dev(1 - y, d, z, y2),
                )

        return carry

    lax.fori_loop(0, REPS, hand_over, 0)

    for plane in range(PLANES):

        @pl.when(off)
        def _():
            landed(qhome.at[plane], q_recv.at[plane])
            landed(kvhome.at[0, plane], kv_recv.at[plane])
            landed(kvhome.at[1, plane], kv_recv.at[PLANES + plane])

        @pl.when(diag)
        def _():
            landed(kvhome.at[other, plane], kv_recv.at[other * PLANES + plane])

    landed(dec.at[1 - y, new_cols], new_recv.at[0])
    for kind in range(2):
        for i in range(REPS):
            mine = (kind == core) & (i == rep) & (off)

            @pl.when(jnp.logical_not(mine))
            def _():
                landed(
                    dec.at[kind, pl.ds(i * PLANE_ROWS, PLANE_ROWS)], p2_recv.at[kind * PLANES + i]
                )

    for source, target, n in ((qhome, q_out, 0), (kvhome, kv_out, 1), (dec, dec_out, 2)):
        pltpu.make_async_copy(source, target, out_sem.at[n]).start()

    landed(new_ref, new_send.at[0])
    for k in range(7):
        landed(block(0, 0), up_send.at[k])
        landed(block(0, 0), down_send.at[k])
    for k in range(16):
        landed(block(0, 0), sib_send.at[k])
    for slot in range(PLANES):
        landed(kvstage.at[0], kv_send.at[slot])

    @pl.when(off)
    def _():
        for h in range(2):
            landed(block(0, h), xs_send.at[h])
        landed(wq_low, w_send.at[0])
        landed(wq_high, w_send.at[1])
        landed(wkv, w_send.at[2])
        for slot in range(PLANES):
            landed(kvstage.at[0], kv_send2.at[slot])
            landed(qstage.at[0], q_send.at[slot])

    def drain(slot, carry):
        high = (z + slot // 2) % PLANES
        low = (z + 2 * PLANES - 1 - slot // 2) % PLANES
        plane = jnp.where(slot % 2 == 0, high, low)

        @pl.when(plane != rep)
        def _():
            landed(kvstage.at[0], p1_send.at[slot])

        for y2 in range(2):
            mine = (1 - y == core) & (slot == rep) & (y == y2)

            @pl.when(jnp.logical_not(mine))
            def _():
                landed(p2.at[0], p2_send.at[2 * slot + y2])

        return carry

    lax.fori_loop(0, PLANES, drain, 0)
    for source, target, n in ((qhome, q_out, 0), (kvhome, kv_out, 1), (dec, dec_out, 2)):
        pltpu.make_async_copy(source, target, out_sem.at[n]).wait()


def attention(
    q_ref,
    kv_ref,
    dec_ref,
    queries_ref,
    lengths_ref,
    pairing_ref,
    assign_ref,
    cache_len_ref,
    prefill_ref,
    decode_ref,
    bias,
):
    core = lax.axis_index("pool")
    rep = lax.axis_index("rep")
    other = 1 - core
    new_cols = pl.ds(CACHE, NEW)
    home_lens = [lengths_ref[core, j, rep] for j in range(4)]
    paired = pairing_ref[core, rep]
    pair_lens = [lengths_ref[other, j, paired] for j in range(4)]

    def column(ref):
        spread = jnp.broadcast_to(ref[...], (ROWS, ROWS))
        here = lax.broadcasted_iota(jnp.int32, (ROWS, ROWS), 0) == lax.broadcasted_iota(
            jnp.int32, (ROWS, ROWS), 1
        )
        picked = jnp.where(here, spread.astype(jnp.float32), 0.0)
        return jnp.sum(picked, axis=1, keepdims=True).astype(jnp.int32)

    member = column(assign_ref)
    limit = column(cache_len_ref)
    lower = jnp.zeros_like(member)
    extent = jnp.zeros_like(member)
    begin = jnp.int32(0)
    for j in range(4):
        lower = jnp.where(member == j, begin, lower)
        extent = jnp.where(member == j, pair_lens[j], extent)
        begin = begin + pair_lens[j]
    upper = lower + jnp.minimum(extent, limit)
    spots = lax.broadcasted_iota(jnp.int32, (ROWS, CACHE), 1)
    visible = jnp.where((spots >= lower) & (spots < upper), 0.0, neg_large)
    new_spot = lax.broadcasted_iota(jnp.int32, (ROWS, NEW), 1)
    row = lax.broadcasted_iota(jnp.int32, (ROWS, NEW), 0)
    for s in range(STEPS):
        rows_here = pl.ds(s * ROWS, ROWS)
        bias[rows_here, pl.ds(0, CACHE)] = visible
        own = (new_spot % ROWS == row) & (new_spot // ROWS <= s)
        bias[rows_here, new_cols] = jnp.where(own, 0.0, neg_large)

    def prefill(i, carry):
        first = jnp.maximum(i - (WINDOW - 1), 0)
        width = WINDOW * PLANE_ROWS
        keys = kv_ref[0, pl.ds(first, WINDOW)].reshape(width, HD)
        values = kv_ref[1, pl.ds(first, WINDOW)].reshape(width, HD)
        row_of = i * PLANE_ROWS + lax.broadcasted_iota(jnp.int32, (PLANE_ROWS, width), 0)
        spot = first * PLANE_ROWS + lax.broadcasted_iota(jnp.int32, (PLANE_ROWS, width), 1)
        begin_of = starts_of(row_of, home_lens)
        mask = jnp.where((spot >= begin_of) & (spot <= row_of), 0.0, neg_large)
        query = q_ref[i].reshape(HEADS * PLANE_ROWS, HD)
        scores = scores_of(query, keys).reshape(HEADS, PLANE_ROWS, width) + mask[None]
        out = softmax_mix(scores.reshape(HEADS * PLANE_ROWS, width), values)
        rows_here = pl.ds(pl.multiple_of(i * PLANE_ROWS, PLANE_ROWS), PLANE_ROWS)
        for h in range(HEADS):
            prefill_ref[rows_here, h * HD : (h + 1) * HD] = out[
                h * PLANE_ROWS : (h + 1) * PLANE_ROWS
            ].astype(jnp.bfloat16)
        return carry

    lax.fori_loop(0, PLANES, prefill, 0)

    for h in range(HEADS):
        scores = scores_of(queries_ref[:, h * HD : (h + 1) * HD], dec_ref[0]) + bias[...]
        decode_ref[:, h * HD : (h + 1) * HD] = softmax_mix(scores, dec_ref[1]).astype(jnp.bfloat16)


def per_device(prompt_states, w_query, w_kv, queries, new_kv, lengths, pairing, assign, cache_len):
    depth = prompt_states.shape[-1]
    q_cols = w_query.shape[1]
    half = np.arange(HD // 2, dtype=np.float32) / np.float32(HD // 2)
    inverse = np.power(np.float32(theta_base), -half).astype(np.float32)
    freq = jnp.asarray(np.concatenate([inverse, inverse])[None, :])
    vmem = pl.BlockSpec(memory_space=pltpu.VMEM)
    smem = pl.BlockSpec(memory_space=pltpu.SMEM)
    anywhere = pl.BlockSpec(memory_space=pl.ANY)
    dma = pltpu.SemaphoreType.DMA
    bf16 = jnp.bfloat16
    lengths_here = lengths.transpose(0, 2, 1)
    q_home, kv_home, caches = pl.pallas_call(
        kernel,
        out_shape=(
            jax.ShapeDtypeStruct((PLANES, HEADS, PLANE_ROWS, HD), bf16),
            jax.ShapeDtypeStruct((2, PLANES, PLANE_ROWS, HD), bf16),
            jax.ShapeDtypeStruct((2, CACHE + NEW, HD), bf16),
        ),
        in_specs=[anywhere, anywhere, anywhere, vmem, smem, smem, vmem],
        out_specs=(anywhere, anywhere, anywhere),
        scratch_shapes=[
            pltpu.VMEM((PLANES, PLANE_ROWS, depth), bf16),
            pltpu.VMEM((depth, q_cols), bf16),
            pltpu.VMEM((depth, HD), bf16),
            pltpu.VMEM((2 * PLANE_ROWS, q_cols + HD), jnp.float32),
            pltpu.VMEM((PLANES, PLANE_ROWS, HD), jnp.float32),
            pltpu.VMEM((PLANES, PLANE_ROWS, HD), jnp.float32),
            pltpu.VMEM((PLANES, HEADS, PLANE_ROWS, HD), bf16),
            pltpu.VMEM((PLANES, HEADS, PLANE_ROWS, HD), bf16),
            pltpu.VMEM((2, PLANES, PLANE_ROWS, HD), bf16),
            pltpu.VMEM((PLANES, PLANE_ROWS, HD), bf16),
            pltpu.VMEM((REPS, PLANE_ROWS, HD), bf16),
            pltpu.VMEM((REPS, PLANE_ROWS, HD), bf16),
            pltpu.VMEM((2, CACHE + NEW, HD), bf16),
            dma((2,)),
            dma((2,)),
            dma((3,)),
            dma((3,)),
            dma((7,)),
            dma((7,)),
            dma((7,)),
            dma((7,)),
            dma((16,)),
            dma((16,)),
            dma((1,)),
            dma((1,)),
            dma((PLANES,)),
            dma((PLANES,)),
            dma((PLANES,)),
            dma((PLANES,)),
            dma((2 * PLANES,)),
            dma((PLANES,)),
            dma((REPS,)),
            dma((2 * REPS,)),
            dma((2 * REPS,)),
            dma((3,)),
        ],
        compiler_params=pltpu.CompilerParams(
            collective_id=0, has_side_effects=True, vmem_limit_bytes=56 * 1024 * 1024
        ),
        cost_estimate=pl.CostEstimate(
            flops=2 * CACHE * depth * (q_cols + HD),
            bytes_accessed=2 * depth * (q_cols + HD + TOK),
            transcendentals=2 * CACHE * HD,
        ),
    )(
        prompt_states.reshape(TOK, depth),
        w_query,
        w_kv,
        new_kv.reshape(NEW, HD),
        lengths_here,
        pairing,
        freq,
    )
    prefill_out, decode_out = pl.pallas_call(
        attention,
        out_shape=(
            jax.ShapeDtypeStruct((CACHE, q_cols), bf16),
            jax.ShapeDtypeStruct((NEW, q_cols), bf16),
        ),
        in_specs=[vmem, vmem, vmem, vmem, smem, smem, vmem, vmem],
        out_specs=(vmem, vmem),
        scratch_shapes=[pltpu.VMEM((NEW, CACHE + NEW), jnp.float32)],
        compiler_params=pltpu.CompilerParams(vmem_limit_bytes=32 * 1024 * 1024),
        cost_estimate=pl.CostEstimate(
            flops=8 * CACHE * CACHE * q_cols,
            bytes_accessed=8 * CACHE * q_cols,
            transcendentals=2 * HEADS * CACHE * CACHE,
        ),
    )(
        q_home,
        kv_home,
        caches,
        queries.reshape(NEW, q_cols),
        lengths_here,
        pairing,
        assign.reshape(1, ROWS),
        cache_len.reshape(1, ROWS),
    )
    return (
        prefill_out.reshape(1, 1, CACHE, q_cols),
        decode_out.reshape(1, 1, STEPS, ROWS, q_cols),
    )


def solution(mesh):
    placed = (
        P("pool", "rep", "tp", None),
        P(None, "tp"),
        P(None, "tp"),
        P("pool", "rep", None, None, "tp"),
        P("pool", "rep", None, None, "tp"),
        P(),
        P(),
        P("pool", "rep", None),
        P("pool", "rep", None),
    )
    return jax.shard_map(
        per_device,
        mesh=mesh,
        in_specs=placed,
        out_specs=(P("pool", "rep", None, "tp"), P("pool", "rep", None, None, "tp")),
        check_vma=False,
    )
```

```python
import functools
import math

import jax
import jax.numpy as jnp
import numpy as np
from jax import lax
from jax.experimental import pallas as pl
from jax.experimental.pallas import tpu as pltpu
from jax.sharding import PartitionSpec as P

HD = 128
PLANES = 8
REPS = 8
HEADS = 4
TOK = 64
PLANE_ROWS = 2 * TOK
WINDOW = 5
STEPS = 4
ROWS = 64
NEW = STEPS * ROWS
CACHE = PLANES * PLANE_ROWS
W_PIECE = 256
W_LOW_PIECES = 3
W_PIECES = 8
K_CHUNK = 2048
WORK = HEADS * PLANE_ROWS

theta_base = 500000.0
neg_large = -1e30
exp_scale = math.log2(math.e) / math.sqrt(HD)


def remote(src, dst, send_sem, recv_sem, device):
    pltpu.make_async_remote_copy(
        src_ref=src,
        dst_ref=dst,
        send_sem=send_sem,
        recv_sem=recv_sem,
        device_id=device,
        device_id_type=pl.DeviceIdType.MESH,
    ).start()


def landed(ref, sem):
    pltpu.make_async_copy(ref, ref, sem).wait()


def scores_of(query, keys):
    return lax.dot_general(
        query, keys, (((1,), (1,)), ((), ())), preferred_element_type=jnp.float32
    )


def kernel(
    x_hbm,
    wq_hbm,
    wkv_hbm,
    queries_ref,
    new_ref,
    lengths_ref,
    pairing_ref,
    assign_ref,
    cache_len_ref,
    cos_hbm,
    sin_hbm,
    prefill_ref,
    decode_ref,
    xg,
    wall,
    accs,
    partial,
    cos_t,
    sin_t,
    bias,
    qhome,
    qstage,
    kvhome,
    kvstage,
    p1,
    p2,
    dec,
    top,
    total,
    mix,
    dec_top,
    dec_total,
    dec_mix,
    tab_sem,
    x0_sem,
    xs_send,
    wl_sem,
    wq_send,
    wq_recv,
    wkv_send,
    wkv_recv,
    wx_send,
    wx_recv,
    up_send,
    up_recv,
    down_send,
    down_recv,
    part_send,
    part_recv,
    new_send,
    new_recv,
    q_send,
    q_recv,
    kv_send,
    kv_send2,
    kv_recv,
    p1_send,
    p1_recv,
    p2_send,
    p2_recv,
):
    core = lax.axis_index("pool")
    rep = lax.axis_index("rep")
    t = lax.axis_index("tp")
    z = t // 2
    y = t % 2
    diag = core == y
    off = core != y
    other = 1 - core

    def dev(c2, g2, z2, y2):
        return (c2, g2, z2 * 2 + y2)

    up_dev = dev(core, rep, (z + 1) % PLANES, y)
    down_dev = dev(core, rep, (z + PLANES - 1) % PLANES, y)
    sibling = dev(other, rep, z, y)
    swap_low = dev(other, rep, z, 1 - y)
    across = dev(core, rep, z, 1 - y)
    across_high = dev(core, (rep + REPS // 2) % REPS, z, 1 - y)
    q_cols = wq_hbm.shape[1]
    parity = rep % 2
    row_of_x = rep // 4 * 4
    right = dev(core, row_of_x + (rep + 1) % 4, z, y)
    left = dev(core, row_of_x + (rep + 3) % 4, z, y)
    half_depth = W_PIECES * W_PIECE

    depth = wall.shape[0]
    cols = q_cols + HD
    own_depth = pl.multiple_of(core * depth, depth)
    other_depth = pl.multiple_of(other * depth, depth)
    mine_cols = pl.ds(pl.multiple_of(core * cols, HD), cols)
    sibling_cols = pl.ds(pl.multiple_of(other * cols, HD), cols)
    far_cols = pl.ds(pl.multiple_of((1 - y) * cols, HD), cols)
    far_q_cols = pl.ds(pl.multiple_of((1 - y) * cols, HD), q_cols)
    far_kv_cols = pl.ds(pl.multiple_of((1 - y) * cols + q_cols, HD), HD)
    near_q_cols = pl.ds(pl.multiple_of(y * cols, HD), q_cols)
    near_kv_cols = pl.ds(pl.multiple_of(y * cols + q_cols, HD), HD)
    half_depth = W_PIECES * W_PIECE

    def depth_rows(half, n):
        return pl.ds(pl.multiple_of(half * half_depth + n * W_PIECE, W_PIECE), W_PIECE)

    def source_rows(half, n):
        start = core * depth + half * half_depth + n * W_PIECE
        return pl.ds(pl.multiple_of(start, W_PIECE), W_PIECE)

    def distance(plane):
        away = (plane + PLANES - z) % PLANES
        return jnp.minimum(away, PLANES - away)

    y_rows = pl.ds(pl.multiple_of(y * TOK, TOK), TOK)
    far_rows = pl.ds(pl.multiple_of((1 - y) * TOK, TOK), TOK)

    def block(slot, h):
        return xg.at[slot, y_rows if h == 0 else far_rows]

    @pl.when(diag)
    def _():
        pltpu.make_async_copy(
            x_hbm.at[:, pl.ds(own_depth, depth)], xg.at[0, y_rows], x0_sem.at[0]
        ).start()

    pltpu.make_async_copy(
        wq_hbm.at[pl.ds(own_depth, depth)], wall.at[:, near_q_cols], wl_sem.at[0]
    ).start()
    pltpu.make_async_copy(
        wkv_hbm.at[pl.ds(own_depth, depth)], wall.at[:, near_kv_cols], wl_sem.at[1]
    ).start()

    pltpu.make_async_copy(cos_hbm, cos_t, tab_sem.at[0]).start()
    pltpu.make_async_copy(sin_hbm, sin_t, tab_sem.at[1]).start()

    barrier = pltpu.get_barrier_semaphore()

    def greet(n, carry):
        c2 = n // 16
        g2 = (n // 2) % 8
        y2 = n % 2
        mine = (c2 == core) & (g2 == rep) & (y2 == y)

        @pl.when(jnp.logical_not(mine))
        def _():
            pl.semaphore_signal(
                barrier, inc=1, device_id=dev(c2, g2, z, y2), device_id_type=pl.DeviceIdType.MESH
            )

        return carry

    lax.fori_loop(0, 32, greet, 0)
    for device in (up_dev, down_dev):
        pl.semaphore_signal(
            barrier, inc=1, device_id=device, device_id_type=pl.DeviceIdType.MESH
        )
    pl.semaphore_wait(barrier, 33)

    @pl.when(diag)
    def _():
        remote(
            x_hbm.at[:, pl.ds(other_depth, depth)],
            xg.at[0, y_rows],
            xs_send.at[0],
            x0_sem.at[0],
            sibling,
        )

    @pl.when(off)
    def _():
        remote(
            x_hbm.at[:, pl.ds(own_depth, depth)],
            xg.at[0, y_rows],
            xs_send.at[0],
            x0_sem.at[1],
            across,
        )
        remote(
            x_hbm.at[:, pl.ds(other_depth, depth)],
            xg.at[0, y_rows],
            xs_send.at[1],
            x0_sem.at[1],
            swap_low,
        )

    for n in range(W_PIECES):
        target = across if n < W_LOW_PIECES else across_high
        remote(
            wq_hbm.at[source_rows(parity, n)],
            wall.at[depth_rows(parity, n), near_q_cols],
            wq_send.at[n],
            wq_recv.at[n],
            target,
        )
        remote(
            wkv_hbm.at[source_rows(parity, n)],
            wall.at[depth_rows(parity, n), near_kv_cols],
            wkv_send.at[n],
            wkv_recv.at[n],
            target,
        )

    def pass_on(pieces):
        for n in pieces:
            rows = depth_rows(parity, n)
            landed(wall.at[rows, far_q_cols], wq_recv.at[n])
            landed(wall.at[rows, far_kv_cols], wkv_recv.at[n])
            target = right if n < W_LOW_PIECES else left
            piece = wall.at[rows, far_cols]
            remote(piece, piece, wx_send.at[n], wx_recv.at[n], target)

    def send_up(src, dst, h, k):
        remote(block(src, h), block(dst, h), up_send.at[k], up_recv.at[k], up_dev)

    def send_down(src, dst, h, k):
        remote(block(src, h), block(dst, h), down_send.at[k], down_recv.at[k], down_dev)

    for h in range(2):
        landed(block(0, h), x0_sem.at[h])
        send_up(0, 1, h, h)
        send_down(0, 2, h, h)

    new_cols = pl.ds(CACHE, NEW)
    remote(new_ref, dec.at[y, new_cols], new_send.at[0], new_recv.at[0], across)
    dec[y, new_cols] = new_ref[...]

    def starts_of(rows, lens):
        end = jnp.int32(0)
        total = jnp.zeros_like(rows)
        for length in lens:
            end = end + length
            total = total + jnp.where(rows >= end, length, 0)
        return total

    work_lens = [lengths_ref[y, j, rep] for j in range(4)]
    home_lens = [lengths_ref[core, j, rep] for j in range(4)]
    paired = pairing_ref[core, rep]
    pair_lens = [lengths_ref[other, j, paired] for j in range(4)]

    work_starts = [jnp.int32(0)]
    for j in range(3):
        work_starts.append(work_starts[j] + work_lens[j])
    landed(cos_t, tab_sem.at[0])
    landed(sin_t, tab_sem.at[1])

    def table_row(ref, row):
        return ref[row // PLANE_ROWS, pl.ds(row % PLANE_ROWS, 1), :]

    start_cos = [table_row(cos_t, row) for row in work_starts]
    start_sin = [table_row(sin_t, row) for row in work_starts]

    def tables(plane, carry):
        rows = plane * PLANE_ROWS + lax.broadcasted_iota(jnp.int32, (PLANE_ROWS, HD), 0)
        cos_b = jnp.broadcast_to(start_cos[0], (PLANE_ROWS, HD))
        sin_b = jnp.broadcast_to(start_sin[0], (PLANE_ROWS, HD))
        for j in range(1, 4):
            later = rows >= work_starts[j]
            cos_b = jnp.where(later, start_cos[j], cos_b)
            sin_b = jnp.where(later, start_sin[j], sin_b)
        cos_a = cos_t[plane]
        sin_a = sin_t[plane]
        cos_t[plane] = cos_a * cos_b + sin_a * sin_b
        sin_t[plane] = sin_a * cos_b - cos_a * sin_b
        return carry

    lax.fori_loop(0, PLANES, tables, 0)

    def column(ref):
        spread = jnp.broadcast_to(ref[...], (ROWS, ROWS))
        here = lax.broadcasted_iota(jnp.int32, (ROWS, ROWS), 0) == lax.broadcasted_iota(
            jnp.int32, (ROWS, ROWS), 1
        )
        picked = jnp.where(here, spread.astype(jnp.float32), 0.0)
        return jnp.sum(picked, axis=1, keepdims=True).astype(jnp.int32)

    member = column(assign_ref)
    limit = column(cache_len_ref)
    lower = jnp.zeros_like(member)
    extent = jnp.zeros_like(member)
    begin = jnp.int32(0)
    for j in range(4):
        lower = jnp.where(member == j, begin, lower)
        extent = jnp.where(member == j, pair_lens[j], extent)
        begin = begin + pair_lens[j]
    upper = lower + jnp.minimum(extent, limit)
    spots = lax.broadcasted_iota(jnp.int32, (ROWS, CACHE), 1)
    visible = jnp.where((spots >= lower) & (spots < upper), 0.0, neg_large)
    new_spot = lax.broadcasted_iota(jnp.int32, (ROWS, NEW), 1)
    row = lax.broadcasted_iota(jnp.int32, (ROWS, NEW), 0)
    for s in range(STEPS):
        rows_here = pl.ds(s * ROWS, ROWS)
        bias[rows_here, pl.ds(0, CACHE)] = visible
        own = (new_spot % ROWS == row) & (new_spot // ROWS <= s)
        bias[rows_here, new_cols] = jnp.where(own, 0.0, neg_large)

    def relay(d, h):
        k = 2 * (d - 1) + h
        low, high = 2 * d - 1, 2 * d
        landed(block(low, h), up_recv.at[k])
        if d < 3:
            send_up(low, low + 2, h, k + 2)
        elif h == 0:
            send_up(low, low + 2, h, 6)
        landed(block(high, h), down_recv.at[k])
        if d < 3:
            send_down(high, high + 2, h, k + 2)
        elif h == 1:
            send_down(high, 7, h, 6)

    def finish_plane(slot, plane, rows):
        cosine = cos_t[plane]
        sine = sin_t[plane]

        def turned(part):
            return part * cosine + pltpu.roll(part, HD // 2, 1) * sine

        heads = [turned(rows[:, h * HD : (h + 1) * HD]).astype(jnp.bfloat16) for h in range(HEADS)]
        raw = rows[:, HEADS * HD :]
        own = jnp.where(core == 0, turned(raw), raw).astype(jnp.bfloat16)
        kvstage[plane] = own

        @pl.when(diag)
        def _():
            for h in range(HEADS):
                qhome[plane, h] = heads[h]
            kvhome[core, plane] = own
            remote(
                kvstage.at[plane],
                kvhome.at[core, plane],
                kv_send.at[slot],
                kv_recv.at[core * PLANES + plane],
                across,
            )

        @pl.when(off)
        def _():
            for h in range(HEADS):
                qstage[slot, h] = heads[h]
            remote(
                kvstage.at[plane],
                kvhome.at[core, plane],
                kv_send.at[slot],
                kv_recv.at[core * PLANES + plane],
                swap_low,
            )
            remote(
                kvstage.at[plane],
                kvhome.at[core, plane],
                kv_send2.at[slot],
                kv_recv.at[core * PLANES + plane],
                sibling,
            )
            remote(qstage.at[slot], qhome.at[plane], q_send.at[slot], q_recv.at[plane], swap_low)

        @pl.when(plane == rep)
        def _():
            p1[rep] = own

        @pl.when(plane != rep)
        def _():
            remote(
                kvstage.at[plane],
                p1.at[rep],
                p1_send.at[slot],
                p1_recv.at[rep],
                dev(core, plane, z, y),
            )

    def project(first, count):
        rows_here = count * PLANE_ROWS

        accs[pl.ds(first, count)] = jnp.zeros((count, PLANE_ROWS, wall.shape[1]), jnp.float32)

        def step(k, carry):
            deep = pl.ds(pl.multiple_of(k * K_CHUNK, K_CHUNK), K_CHUNK)
            rows = xg[pl.ds(first, count), :, deep].reshape(rows_here, K_CHUNK)
            out = jnp.dot(rows, wall[deep, :], preferred_element_type=jnp.float32)
            accs[pl.ds(first, count)] += out.reshape(count, PLANE_ROWS, wall.shape[1])
            return carry

        lax.fori_loop(0, depth // K_CHUNK, step, 0)
        for slot in range(first, first + count):
            remote(
                accs.at[slot, :, sibling_cols],
                partial.at[slot],
                part_send.at[slot],
                part_recv.at[slot],
                sibling,
            )

    def finish(slots):
        for slot, away in slots:
            landed(partial.at[slot], part_recv.at[slot])
            rows = accs[slot, :, mine_cols] + partial[slot]
            finish_plane(slot, (z + PLANES + away) % PLANES, rows)

    cache_rows = pl.ds(pl.multiple_of(rep * PLANE_ROWS, PLANE_ROWS), PLANE_ROWS)

    def hand_over(nearest, farthest):
        here = distance(rep)

        @pl.when((here >= nearest) & (here <= farthest))
        def _():
            for g2 in range(REPS):

                @pl.when(rep != g2)
                def _():
                    landed(p1.at[g2], p1_recv.at[g2])

            def give(d, carry):
                p2[d] = p1[pairing_ref[1 - y, d]]
                for y2 in range(2):
                    mine = (1 - y == core) & (d == rep) & (y == y2)

                    @pl.when(mine)
                    def _():
                        dec[core, cache_rows] = p2[d]

                    @pl.when(jnp.logical_not(mine))
                    def _():
                        remote(
                            p2.at[d],
                            dec.at[core, cache_rows],
                            p2_send.at[2 * d + y2],
                            p2_recv.at[core * PLANES + rep],
                            dev(1 - y, d, z, y2),
                        )

                return carry

            lax.fori_loop(0, REPS, give, 0)

    def home_landed(away):
        plane = (z + PLANES + away) % PLANES

        @pl.when(off)
        def _():
            landed(qhome.at[plane], q_recv.at[plane])
            landed(kvhome.at[0, plane], kv_recv.at[plane])
            landed(kvhome.at[1, plane], kv_recv.at[PLANES + plane])

        @pl.when(diag)
        def _():
            landed(kvhome.at[other, plane], kv_recv.at[other * PLANES + plane])

    def attend(i, planes, fresh):
        width = len(planes) * PLANE_ROWS
        row_of = i * PLANE_ROWS + lax.broadcasted_iota(jnp.int32, (PLANE_ROWS, 1), 0)
        lanes = lax.broadcasted_iota(jnp.int32, (PLANE_ROWS, PLANE_ROWS), 1)
        spot = jnp.concatenate([lanes + j * PLANE_ROWS for j in planes], axis=1)
        keys = jnp.concatenate([kvhome[0, j] for j in planes], axis=0)
        values = jnp.concatenate([kvhome[1, j] for j in planes], axis=0)
        begin_of = starts_of(row_of, home_lens)
        mask = jnp.where((spot >= begin_of) & (spot <= row_of), 0.0, neg_large)
        scores = scores_of(qhome[i].reshape(WORK, HD), keys)
        scores = (scores.reshape(HEADS, PLANE_ROWS, width) + mask[None]).reshape(WORK, width)
        peak = jnp.max(scores, axis=-1, keepdims=True)
        if not fresh:
            before = top[i]
            peak = jnp.maximum(before[:, :1], peak)
            fade = jnp.exp2((before - peak) * exp_scale)
        weights = jnp.exp2((scores - peak) * exp_scale)
        summed = jnp.sum(weights, axis=-1, keepdims=True)
        mixed = jnp.dot(weights.astype(jnp.bfloat16), values, preferred_element_type=jnp.float32)
        if fresh:
            total[i] = jnp.broadcast_to(summed, (WORK, HD))
            mix[i] = mixed
        else:
            total[i] = total[i] * fade + summed
            mix[i] = mix[i] * fade + mixed
        top[i] = jnp.broadcast_to(peak, (WORK, HD))

    def plane_at(away):
        return (z + PLANES + away) % PLANES

    def attend_near():
        planes = [plane_at(away) for away in near]

        def one(n, carry):
            attend((z + PLANES - 2 + n) % PLANES, planes, True)
            return carry

        lax.fori_loop(0, 5, one, 0)

    def attend_third():
        planes = [plane_at(-3), plane_at(3)]

        def one(n, carry):
            attend((z + PLANES - 2 + n) % PLANES, planes, False)
            return carry

        lax.fori_loop(0, 5, one, 0)

        def two(n, carry):
            attend((z + PLANES - 3 + 6 * n) % PLANES, planes + [plane_at(a) for a in near], True)
            return carry

        lax.fori_loop(0, 2, two, 0)

    def attend_last():
        last = plane_at(4)
        first = jnp.maximum(last - (WINDOW - 1), 0)
        attend(last, [first + n for n in range(WINDOW)], True)

        def one(n, carry):
            i = last + 1 + n

            @pl.when(i < PLANES)
            def _():
                attend(i, [last], False)

            return carry

        lax.fori_loop(0, WINDOW - 1, one, 0)

    def settle(late):
        def one(i, carry):
            after = i - (z + 4) % PLANES
            needs_last = (after >= 0) & (after < WINDOW)

            @pl.when(needs_last if late else jnp.logical_not(needs_last))
            def _():
                out = mix[i] / total[i]
                rows_here = pl.ds(pl.multiple_of(i * PLANE_ROWS, PLANE_ROWS), PLANE_ROWS)
                for h in range(HEADS):
                    prefill_ref[rows_here, h * HD : (h + 1) * HD] = out[
                        h * PLANE_ROWS : (h + 1) * PLANE_ROWS
                    ].astype(jnp.bfloat16)

            return carry

        lax.fori_loop(0, PLANES, one, 0)

    def caches_landed(aways):
        for away in aways:
            plane = (z + PLANES + away) % PLANES
            rows_here = pl.ds(pl.multiple_of(plane * PLANE_ROWS, PLANE_ROWS), PLANE_ROWS)
            for kind in range(2):
                mine = (kind == core) & (plane == rep) & off

                @pl.when(jnp.logical_not(mine))
                def _():
                    landed(dec.at[kind, rows_here], p2_recv.at[kind * PLANES + plane])

    def cache_slices(aways):
        slices = []
        for away in aways:
            plane = (z + PLANES + away) % PLANES
            slices.append(pl.ds(pl.multiple_of(plane * PLANE_ROWS, PLANE_ROWS), PLANE_ROWS))
        return slices

    def decode_scores(h, slices):
        query = queries_ref[:, h * HD : (h + 1) * HD]
        keys = jnp.concatenate([dec[0, piece] for piece in slices], axis=0)
        mask = jnp.concatenate([bias[:, piece] for piece in slices], axis=1)
        values = jnp.concatenate([dec[1, piece] for piece in slices], axis=0)
        return scores_of(query, keys) + mask, values

    def decode_first(aways):
        slices = cache_slices(aways) + [new_cols]
        for h in range(HEADS):
            scores, values = decode_scores(h, slices)
            peak = jnp.max(scores, axis=-1, keepdims=True)
            weights = jnp.exp2((scores - peak) * exp_scale)
            dec_top[h] = jnp.broadcast_to(peak, (NEW, HD))
            dec_total[h] = jnp.broadcast_to(
                jnp.sum(weights, axis=-1, keepdims=True), (NEW, HD)
            )
            dec_mix[h] = jnp.dot(
                weights.astype(jnp.bfloat16), values, preferred_element_type=jnp.float32
            )

    def decode_last(aways):
        slices = cache_slices(aways)
        for h in range(HEADS):
            scores, values = decode_scores(h, slices)
            before = dec_top[h]
            peak = jnp.maximum(before, jnp.max(scores, axis=-1, keepdims=True))
            fade = jnp.exp2((before - peak) * exp_scale)
            weights = jnp.exp2((scores - peak[:, :1]) * exp_scale)
            whole = dec_total[h] * fade + jnp.sum(weights, axis=-1, keepdims=True)
            mixed = dec_mix[h] * fade + jnp.dot(
                weights.astype(jnp.bfloat16), values, preferred_element_type=jnp.float32
            )
            decode_ref[:, h * HD : (h + 1) * HD] = (mixed / whole).astype(jnp.bfloat16)

    near = (0, -1, 1, -2, 2)
    relay(1, 0)
    pass_on((3, 4))
    relay(1, 1)
    pass_on((0, 5, 1, 6))
    relay(2, 0)
    pass_on((2, 7))
    relay(2, 1)
    landed(wall.at[:, near_q_cols], wl_sem.at[0])
    landed(wall.at[:, near_kv_cols], wl_sem.at[1])
    for n in range(W_PIECES):
        landed(wall.at[depth_rows(1 - parity, n), far_cols], wx_recv.at[n])

    project(0, 5)
    relay(3, 0)
    finish(((0, 0), (1, -1), (2, 1), (3, -2), (4, 2)))
    hand_over(0, 2)
    for away in near:
        home_landed(away)
    attend_near()
    relay(3, 1)
    project(5, 2)
    finish(((5, -3), (6, 3)))
    hand_over(3, 3)
    for away in (-3, 3):
        home_landed(away)
    attend_third()
    settle(False)
    landed(block(7, 0), up_recv.at[6])
    landed(block(7, 1), down_recv.at[6])
    project(7, 1)
    finish(((7, 4),))
    hand_over(4, 4)
    landed(dec.at[1 - y, new_cols], new_recv.at[0])
    caches_landed(near)
    decode_first(near)
    home_landed(4)
    attend_last()
    settle(True)
    far = (-3, 3, 4)
    caches_landed(far)
    decode_last(far)

    landed(new_ref, new_send.at[0])
    for k in range(7):
        landed(block(0, 0), up_send.at[k])
        landed(block(0, 0), down_send.at[k])
    landed(block(0, 0), xs_send.at[0])
    for slot in range(PLANES):
        landed(kvstage.at[0], kv_send.at[slot])
        landed(partial.at[0], part_send.at[slot])
    for n in range(W_PIECES):
        rows = depth_rows(0, n)
        landed(wall.at[rows, near_q_cols], wq_send.at[n])
        landed(wall.at[rows, near_kv_cols], wkv_send.at[n])
        landed(wall.at[rows, far_cols], wx_send.at[n])

    @pl.when(off)
    def _():
        landed(block(0, 0), xs_send.at[1])
        for slot in range(PLANES):
            landed(kvstage.at[0], kv_send2.at[slot])
            landed(qstage.at[0], q_send.at[slot])

    def drain(slot, carry):
        odd = slot % 2
        step = (slot + odd) // 2
        plane = jnp.where(odd == 0, (z + step) % PLANES, (z + PLANES - step) % PLANES)

        @pl.when(plane != rep)
        def _():
            landed(kvstage.at[0], p1_send.at[slot])

        for y2 in range(2):
            mine = (1 - y == core) & (slot == rep) & (y == y2)

            @pl.when(jnp.logical_not(mine))
            def _():
                landed(p2.at[0], p2_send.at[2 * slot + y2])

        return carry

    lax.fori_loop(0, PLANES, drain, 0)


def hand_out(prefill_in, decode_in, prefill_ref, decode_ref):
    prefill_ref[...] = prefill_in[...]
    decode_ref[...] = decode_in[...]


def per_device(prompt_states, w_query, w_kv, queries, new_kv, lengths, pairing, assign, cache_len):
    depth = prompt_states.shape[-1]
    q_cols = w_query.shape[1]
    powers = np.arange(HD // 2, dtype=np.float32) / np.float32(HD // 2)
    inverse = np.power(np.float32(theta_base), -powers).astype(np.float64)
    angle = np.arange(CACHE, dtype=np.float64)[:, None] * inverse[None, :]
    cosine, sine = np.cos(angle), np.sin(angle)
    table_shape = (PLANES, PLANE_ROWS, HD)
    cos_table = np.concatenate([cosine, cosine], axis=1).astype(np.float32).reshape(table_shape)
    sin_table = np.concatenate([-sine, sine], axis=1).astype(np.float32).reshape(table_shape)
    vmem = pl.BlockSpec(memory_space=pltpu.VMEM)
    smem = pl.BlockSpec(memory_space=pltpu.SMEM)
    anywhere = pl.BlockSpec(memory_space=pl.ANY)
    dma = pltpu.SemaphoreType.DMA
    bf16 = jnp.bfloat16
    prefill_out, decode_out = pl.pallas_call(
        kernel,
        out_shape=(
            jax.ShapeDtypeStruct((CACHE, q_cols), bf16),
            jax.ShapeDtypeStruct((NEW, q_cols), bf16),
        ),
        in_specs=[anywhere, anywhere, anywhere, vmem, vmem, smem, smem, vmem, vmem, anywhere, anywhere],
        out_specs=(vmem, vmem),
        scratch_shapes=[
            pltpu.VMEM((PLANES, PLANE_ROWS, depth // 2), bf16),
            pltpu.VMEM((depth // 2, 2 * (q_cols + HD)), bf16),
            pltpu.VMEM((PLANES, PLANE_ROWS, 2 * (q_cols + HD)), jnp.float32),
            pltpu.VMEM((PLANES, PLANE_ROWS, q_cols + HD), jnp.float32),
            pltpu.VMEM((PLANES, PLANE_ROWS, HD), jnp.float32),
            pltpu.VMEM((PLANES, PLANE_ROWS, HD), jnp.float32),
            pltpu.VMEM((NEW, CACHE + NEW), jnp.float32),
            pltpu.VMEM((PLANES, HEADS, PLANE_ROWS, HD), bf16),
            pltpu.VMEM((PLANES, HEADS, PLANE_ROWS, HD), bf16),
            pltpu.VMEM((2, PLANES, PLANE_ROWS, HD), bf16),
            pltpu.VMEM((PLANES, PLANE_ROWS, HD), bf16),
            pltpu.VMEM((REPS, PLANE_ROWS, HD), bf16),
            pltpu.VMEM((REPS, PLANE_ROWS, HD), bf16),
            pltpu.VMEM((2, CACHE + NEW, HD), bf16),
            pltpu.VMEM((PLANES, WORK, HD), jnp.float32),
            pltpu.VMEM((PLANES, WORK, HD), jnp.float32),
            pltpu.VMEM((PLANES, WORK, HD), jnp.float32),
            pltpu.VMEM((HEADS, NEW, HD), jnp.float32),
            pltpu.VMEM((HEADS, NEW, HD), jnp.float32),
            pltpu.VMEM((HEADS, NEW, HD), jnp.float32),
            dma((2,)),
            dma((2,)),
            dma((2,)),
            dma((2,)),
            dma((W_PIECES,)),
            dma((W_PIECES,)),
            dma((W_PIECES,)),
            dma((W_PIECES,)),
            dma((W_PIECES,)),
            dma((W_PIECES,)),
            dma((7,)),
            dma((7,)),
            dma((7,)),
            dma((7,)),
            dma((PLANES,)),
            dma((PLANES,)),
            dma((1,)),
            dma((1,)),
            dma((PLANES,)),
            dma((PLANES,)),
            dma((PLANES,)),
            dma((PLANES,)),
            dma((2 * PLANES,)),
            dma((PLANES,)),
            dma((REPS,)),
            dma((2 * REPS,)),
            dma((2 * REPS,)),
        ],
        compiler_params=pltpu.CompilerParams(
            collective_id=0, has_side_effects=True, vmem_limit_bytes=56 * 1024 * 1024
        ),
        cost_estimate=pl.CostEstimate(
            flops=2 * CACHE * depth * (q_cols + HD) + 8 * CACHE * CACHE * q_cols,
            bytes_accessed=2 * depth * (q_cols + HD + TOK),
            transcendentals=2 * HEADS * CACHE * CACHE,
        ),
    )(
        prompt_states.reshape(TOK, depth),
        w_query,
        w_kv,
        queries.reshape(NEW, q_cols),
        new_kv.reshape(NEW, HD),
        lengths.transpose(0, 2, 1),
        pairing,
        assign.reshape(1, ROWS),
        cache_len.reshape(1, ROWS),
        jnp.asarray(cos_table),
        jnp.asarray(sin_table),
    )
    prefill_out, decode_out = pl.pallas_call(
        hand_out,
        out_shape=(
            jax.ShapeDtypeStruct((CACHE, q_cols), bf16),
            jax.ShapeDtypeStruct((NEW, q_cols), bf16),
        ),
        in_specs=[vmem, vmem],
        out_specs=(vmem, vmem),
        compiler_params=pltpu.CompilerParams(vmem_limit_bytes=62 * 1024 * 1024),
    )(prefill_out, decode_out)
    return (
        prefill_out.reshape(1, 1, CACHE, q_cols),
        decode_out.reshape(1, 1, STEPS, ROWS, q_cols),
    )


def solution(mesh):
    placed = (
        P("pool", "rep", "tp", None),
        P(None, "tp"),
        P(None, "tp"),
        P("pool", "rep", None, None, "tp"),
        P("pool", "rep", None, None, "tp"),
        P(),
        P(),
        P("pool", "rep", None),
        P("pool", "rep", None),
    )
    return jax.shard_map(
        per_device,
        mesh=mesh,
        in_specs=placed,
        out_specs=(P("pool", "rep", None, "tp"), P("pool", "rep", None, None, "tp")),
        check_vma=False,
    )
```
